512 devices in a mesh: outer: 64 (over y_lo, z, core), inner: 8 (over y_hi, x).
Axes of the slice: x: 4, y: 8 (y_hi: 2, y_lo: 4; y = y_hi * 4 + y_lo), z: 8, core: 2. Of those that a mesh axis runs over, the one named last changes fastest.
Arguments:
- queries: float32 [64, 1024, 256], P('outer', 'inner'), may hold values from -120 to 120
- key_rows: float32 [64, 1024, 128], P('outer', 'inner'), may hold values from -4 to 4
- value_rows: float32 [64, 1024, 128], P('outer', 'inner'), may hold values from -6 to 6
- cotangent: float32 [64, 1024, 256], P('outer', 'inner'), may hold values from -6 to 6
- block_order: int32 [32], replicated, may hold values from 0 to 31, each once
Outputs:
- attended: float32 [64, 1024, 256], P('outer', 'inner')
- query_grad: float32 [64, 1024, 256], P('outer', 'inner')
- key_grad: float32 [64, 1024, 128], P('outer', 'inner')
- value_grad: float32 [64, 1024, 128], P('outer', 'inner')
The draws below stay inside these ranges and needn't reach their ends.
Inputs may be any that keep to these rules, and one draw needn't show every extreme that they name: block_order is a permutation; stored block b of every sequence holds positions block_order[b] * 128 to block_order[b] * 128 + 127.
All inputs are finite; a program needn't handle non-finite values.
Results may differ from the reference program's by a relative error of at most 0.00055.
Values sent between devices are 32-bit elements; how exact they have to be, the bound alone decides.
A program may use at most 64 MiB of HBM per device.

```python
import jax
import jax.numpy as jnp
from jax import lax

HD = 128
HEADS = 2
TOK_DEV = 128
GROUPS = 4
SEQS = 16
SLAB = 1024
NBLK = 32


def shared_keys(key):
    return jnp.clip(jax.random.normal(key, (GROUPS * SEQS, SLAB, HD), jnp.float32), -4.0, 4.0)


def draw_key_rows(key, part):
    drawn = shared_keys(key)
    return drawn


def draw_queries(key, part):
    key = jax.random.fold_in(key, 13)
    first = jax.random.fold_in(key, 0)
    drawn = jnp.clip(jax.random.normal(first, (GROUPS * SEQS, SLAB, HEADS * HD), jnp.float32), -4.0, 4.0)
    return drawn


def level_of(key, shape, cuts, smallest, largest):
    def one(position, parts):
        heights = jax.random.uniform(jax.random.fold_in(jax.random.fold_in(key, 6), position), (parts,), jnp.float32, smallest / len(cuts), largest / len(cuts))
        return jnp.repeat(jnp.exp(heights), shape[position] // parts).reshape((-1,) + (1,) * (len(shape) - position - 1))

    gain = one(*cuts[0])
    for cut in cuts[1:]:
        gain = gain * one(*cut)
    return gain


def scatter_about(own_key, dims, width, limit, shards=(), kind=jnp.bfloat16):
    result = width * jax.random.normal(own_key, dims, jnp.float32)
    if shards:
        result = result * level_of(own_key, dims, shards, -0.22, 0.18)
    return jnp.clip(result, -limit, limit).astype(kind)


def setup_inputs(seed: int = 0) -> dict:
    arg_keys = jax.random.split(jax.random.key(seed), 6)
    return {
        "queries": draw_queries(jax.random.fold_in(arg_keys[5], 71), 0),
        "key_rows": draw_key_rows(jax.random.fold_in(arg_keys[5], 71), 0),
        "value_rows": scatter_about(arg_keys[2], (GROUPS * SEQS, SLAB, HD), 1.0, 6.0, ((0, 64), (1, 8)), jnp.float32),
        "cotangent": scatter_about(arg_keys[3], (GROUPS * SEQS, SLAB, HEADS * HD), 1.0, 6.0, ((0, 64), (1, 8)), jnp.float32),
        "block_order": jax.random.permutation(arg_keys[4], NBLK).astype(jnp.int32),
    }


HIGH = lax.Precision.HIGHEST

def to_sequences(array):
    columns = array.shape[-1]
    return array.reshape(GROUPS, SEQS, SLAB, columns).transpose(1, 0, 2, 3).reshape(SEQS, GROUPS * SLAB, columns)

def from_sequences(array):
    columns = array.shape[-1]
    return array.reshape(SEQS, GROUPS, SLAB, columns).transpose(1, 0, 2, 3).reshape(GROUPS * SEQS, SLAB, columns)

def attend(query_seq, key_seq, value_seq, positions):
    length = key_seq.shape[0]
    by_head = query_seq.reshape(length, HEADS, HD)
    scores = jnp.einsum('qhd,kd->hqk', by_head, key_seq, precision=HIGH) * HD ** (-0.5)
    visible = positions[None, :] <= positions[:, None]
    scores = jnp.where(visible[None], scores, -jnp.inf)
    weights = jax.nn.softmax(scores, axis=-1)
    mixed = jnp.einsum('hqk,kd->qhd', weights, value_seq, precision=HIGH)
    return mixed.reshape(length, HEADS * HD)

def reference(queries, key_rows, value_rows, cotangent, block_order):
    offsets = jnp.arange(TOK_DEV, dtype=jnp.int32)
    positions = (block_order.astype(jnp.int32)[:, None] * TOK_DEV + offsets[None, :]).reshape(-1).astype(jnp.int32)

    def one_sequence(inputs):
        query_seq, key_seq, value_seq, grad_seq = inputs

        def forward(first, second, third):
            return attend(first, second, third, positions)
        output, pullback = jax.vjp(forward, query_seq, key_seq, value_seq)
        grads = pullback(grad_seq)
        return (output, grads[0], grads[1], grads[2])
    outputs = lax.map(one_sequence, (to_sequences(queries), to_sequences(key_rows), to_sequences(value_rows), to_sequences(cotangent)))
    return (from_sequences(outputs[0]), from_sequences(outputs[1]), from_sequences(outputs[2]), from_sequences(outputs[3]))
```

```python
import jax
import jax.numpy as jnp
from jax import lax
from jax.experimental import pallas as pl
from jax.experimental.pallas import tpu as pltpu
from jax.sharding import PartitionSpec as P

HD = 128
HEADS = 2
GROUPS = 4
TOK = 128
NX = 4
NY = 8
QCOLS = HEADS * TOK
ALLQ = NX * QCOLS
ALLK = NY * TOK
HALF = TOK // 2
SCALE = HD ** (-0.5)
LOG2E = 1.4426950408889634
LN2 = 0.6931471805599453
FAR = -1e30
MESH = pl.DeviceIdType.MESH
F32 = jnp.float32
BF16 = jnp.bfloat16

AT = (0, 1, 7, 2, 6, 3, 5, 4)
PLACE = tuple(AT.index(r) for r in range(NY))
CHUNK = 2 * TOK


def split2(value):
    high = value.astype(BF16)
    return high, (value - high.astype(F32)).astype(BF16)


def split3(value):
    high = value.astype(BF16)
    rest = value - high.astype(F32)
    mid = rest.astype(BF16)
    return high, mid, (rest - mid.astype(F32)).astype(BF16)


def matmul(left, right):
    return jnp.dot(left, right, preferred_element_type=F32)


def matmul_nt(left, right):
    return lax.dot_general(left, right, (((1,), (1,)), ((), ())), preferred_element_type=F32)


def fold_rows(value, combine):
    return combine(value.reshape(value.shape[0] // 8, 8, value.shape[1]), axis=0)


def kernel(
    order, q_hbm, k_hbm, v_hbm, g_hbm, o_out, dq_out, dk_out, dv_out,
    q_own, g_own, q_t, g_t, keys, vals, qs, gs, kp, vp, kt, vt, qf, gf,
    scores, gw, p_hi, p_lo, t_hi, t_lo, max8, sum8, dot8, stats, dots, scaled,
    dv_part, dk_part, o_part, dq_part, dv_in, dv_half, dk_in, dk_half, o_in, o_half, dq_in, dq_half,
    local_sem, qx_s, qx_r, gx_s, gx_r, ky_s, ky_r, vy_s, vy_r, st_s, st_r, rd_s, rd_r,
    dvy_s, dvy_r, dky_s, dky_r, ox_s, ox_r, dqx_s, dqx_r,
):
    seqs = lax.axis_size("outer") // GROUPS
    outer = lax.axis_index("outer")
    inner = lax.axis_index("inner")
    seq = lax.rem(outer, seqs)
    x = lax.rem(inner, NX)
    y = (inner // NX) * GROUPS + outer // seqs

    def device(at_x, at_y):
        return (lax.rem(at_y, GROUPS) * seqs + seq, (at_y // GROUPS) * NX + at_x)

    def along_x(step):
        return device(lax.rem(x + step + NX, NX), y)

    def along_y(step):
        return device(x, lax.rem(y + step + NY, NY))

    def position(at_x, at_y):
        return order[lax.rem(at_y, GROUPS) * (NX * NY // GROUPS) + (at_y // GROUPS) * NX + at_x]

    def remote(src, dst, send, recv, where):
        return pltpu.make_async_remote_copy(
            src_ref=src, dst_ref=dst, send_sem=send, recv_sem=recv, device_id=where, device_id_type=MESH
        )

    up, down, right, left, across = along_y(1), along_y(-1), along_x(1), along_x(-1), along_x(2)
    peers = (right, across, left)

    loads = [
        pltpu.make_async_copy(q_hbm.at[0], q_own, local_sem.at[0]),
        pltpu.make_async_copy(g_hbm.at[0], g_own, local_sem.at[1]),
        pltpu.make_async_copy(k_hbm.at[0], keys.at[0], local_sem.at[2]),
        pltpu.make_async_copy(v_hbm.at[0], vals.at[0], local_sem.at[3]),
    ]
    for load in loads:
        load.start()
    barrier = pltpu.get_barrier_semaphore()
    for peer in (up, down, right, left, across):
        pl.semaphore_signal(barrier, inc=1, device_id=peer, device_id_type=MESH)
    loads[0].wait()
    for h in range(HEADS):
        q_t[0, :, h * TOK:(h + 1) * TOK] = q_own[:, h * HD:(h + 1) * HD].T * (SCALE * LOG2E)
    loads[1].wait()
    for h in range(HEADS):
        g_t[0, :, h * TOK:(h + 1) * TOK] = g_own[:, h * HD:(h + 1) * HD].T
    loads[2].wait()
    loads[3].wait()
    pl.semaphore_wait(barrier, 5)

    def ring_y(buf, send, recv):
        copies = {}
        for j in range(4):
            for d, (sign, where) in enumerate(((1, up), (-1, down))):
                src, dst = PLACE[(sign * j) % NY], PLACE[(sign * (j + 1)) % NY]
                rows = pl.ds(0, TOK) if j < 3 else pl.ds(d * HALF, HALF)
                n = 2 * j + d
                copies[j, d] = remote(buf.at[src, rows], buf.at[dst, rows], send.at[n], recv.at[n], where)
        return copies

    def ring_x(buf, send, recv):
        copies = {}
        for d, where in enumerate((right, left)):
            near = 1 if d == 0 else 3
            copies[0, d] = remote(buf.at[0], buf.at[near], send.at[d], recv.at[d], where)
            rows = pl.ds(d * HALF, HALF)
            copies[1, d] = remote(buf.at[near, rows], buf.at[2, rows], send.at[2 + d], recv.at[2 + d], where)
        return copies

    k_go, v_go = ring_y(keys, ky_s, ky_r), ring_y(vals, vy_s, vy_r)
    q_go, g_go = ring_x(q_t, qx_s, qx_r), ring_x(g_t, gx_s, gx_r)
    everything = [*k_go.values(), *v_go.values(), *q_go.values(), *g_go.values()]

    def pass_on(copies, j, last):
        for d in range(2):
            copies[j - 1, d].wait_recv()
            if j <= last:
                copies[j, d].start()

    def ready_query(s):
        cols = pl.ds(s * QCOLS, QCOLS)
        q0, q1, q2 = split3(q_t[s])
        for n, piece in enumerate((q0, q1, q0, q1, q0, q2)):
            qs[n * HD:(n + 1) * HD, cols] = piece

    def ready_cotangent(s):
        cols = pl.ds(s * QCOLS, QCOLS)
        g0, g1 = split2(g_t[s])
        for n, piece in enumerate((g0, g1, g0)):
            gs[n * HD:(n + 1) * HD, cols] = piece

    def ready_key(place):
        rows = pl.ds(place * TOK, TOK)
        k0, k1, k2 = split3(keys[place])
        for n, piece in enumerate((k0, k0, k1, k1, k2, k0)):
            kp[rows, n * HD:(n + 1) * HD] = piece
        high, low = split2(keys[place].T)
        kt[0:HD, rows] = high
        kt[HD:2 * HD, rows] = low

    def ready_value(place):
        rows = pl.ds(place * TOK, TOK)
        v0, v1 = split2(vals[place])
        for n, piece in enumerate((v0, v0, v1)):
            vp[rows, n * HD:(n + 1) * HD] = piece
        high, low = split2(vals[place].T)
        vt[0:HD, rows] = high
        vt[HD:2 * HD, rows] = low

    def score_chunk(c):
        rows = pl.ds(c * CHUNK, CHUNK)
        for s in range(NX):
            cols = pl.ds(s * QCOLS, QCOLS)
            query_at = position(lax.rem(x - s + NX, NX), y)
            tile = matmul(kp[rows, :], qs[:, cols])
            parts = []
            for n in range(2):
                r = AT[2 * c + n]
                part = tile[n * TOK:(n + 1) * TOK]
                if r == 0 and s == 0:
                    key_at = lax.broadcasted_iota(jnp.int32, (TOK, QCOLS), 0)
                    token = lax.rem(lax.broadcasted_iota(jnp.int32, (TOK, QCOLS), 1), TOK)
                    part = jnp.where(key_at <= token, part, FAR)
                else:
                    seen = position(x, lax.rem(y - r + NY, NY)) <= query_at
                    part = part + jnp.where(seen, 0.0, FAR).astype(F32)
                parts.append(part)
            for n, part in enumerate(parts):
                scores[c * CHUNK + n * TOK:c * CHUNK + (n + 1) * TOK, cols] = part
            top = jnp.maximum(fold_rows(parts[0], jnp.max), fold_rows(parts[1], jnp.max))
            max8[:, cols] = top if c == 0 else jnp.maximum(max8[:, cols], top)

    for d in range(2):
        k_go[0, d].start()
        q_go[0, d].start()
    for d in range(2):
        v_go[0, d].start()
        g_go[0, d].start()
    ready_query(0)
    ready_key(0)
    ready_cotangent(0)
    ready_value(0)

    pass_on(k_go, 1, 3)
    ready_key(1)
    ready_key(2)
    pass_on(q_go, 1, 1)
    ready_query(1)
    ready_query(3)
    pass_on(v_go, 1, 3)
    pass_on(k_go, 2, 3)
    ready_key(3)
    ready_key(4)
    pass_on(g_go, 1, 1)
    pass_on(q_go, 2, 1)
    ready_query(2)
    score_chunk(0)
    pass_on(v_go, 2, 3)
    score_chunk(1)
    pass_on(k_go, 3, 3)
    ready_key(5)
    ready_key(6)
    score_chunk(2)
    pass_on(v_go, 3, 3)
    pass_on(k_go, 4, 3)
    ready_key(7)
    score_chunk(3)

    top = jnp.max(max8[...], axis=0, keepdims=True)
    for c in range(NY // 2):
        rows = pl.ds(c * CHUNK, CHUNK)
        for s in range(NX):
            cols = pl.ds(s * QCOLS, QCOLS)
            weight = jnp.exp2(scores[rows, cols] - top[:, s * QCOLS:(s + 1) * QCOLS])
            scores[rows, cols] = weight
            high, low = split2(weight)
            p_hi[rows, cols] = high
            p_lo[rows, cols] = low
            part = fold_rows(weight, jnp.sum)
            sum8[:, cols] = part if c == 0 else sum8[:, cols] + part
    stats[0, 0:1, :] = top
    stats[0, 1:2, :] = jnp.sum(sum8[...], axis=0, keepdims=True)
    st_go = [
        remote(stats.at[0], stats.at[n + 1], st_s.at[n], st_r.at[n], peers[n]) for n in range(NX - 1)
    ]
    for copy in st_go:
        copy.start()

    pass_on(g_go, 2, 1)
    for s in (1, 3, 2):
        ready_cotangent(s)
    for place in range(1, 5):
        ready_value(place)

    def weigh_chunk(c):
        rows = pl.ds(c * CHUNK, CHUNK)
        for s in range(NX):
            cols = pl.ds(s * QCOLS, QCOLS)
            tile = matmul(vp[rows, :], gs[:, cols])
            gw[rows, cols] = tile
            part = fold_rows(tile * scores[rows, cols], jnp.sum)
            dot8[:, cols] = part if c == 0 else dot8[:, cols] + part

    weigh_chunk(0)
    weigh_chunk(1)

    def aligned(row, n):
        cut = ALLQ - (n + 1) * QCOLS
        return jnp.concatenate([row[:, cut:], row[:, :cut]], axis=1)

    for copy in st_go:
        copy.wait_recv()
    tops = [aligned(stats[n + 1, 0:1, :], n) for n in range(NX - 1)]
    whole_top = jnp.maximum(jnp.maximum(top, tops[0]), jnp.maximum(tops[1], tops[2]))
    own_factor = jnp.exp2(top - whole_top)
    total = own_factor * stats[0, 1:2, :]
    for n in range(NX - 1):
        total = total + jnp.exp2(tops[n] - whole_top) * aligned(stats[n + 1, 1:2, :], n)
    factor = own_factor / total
    scaled[...] = factor

    for s in range(NX):
        cols = pl.ds(s * QCOLS, QCOLS)
        row = scaled[:, cols]
        high, low = split2(g_t[s] * row)
        gf[0:HD, cols] = high
        gf[HD:2 * HD, cols] = low
        high, low = split2(q_t[s] * row)
        qf[0:HD, cols] = high
        qf[HD:2 * HD, cols] = low

    def key_side(c, high, low, right_side, part):
        rows = pl.ds(c * CHUNK, CHUNK)
        both = matmul_nt(high[rows, :], right_side[...]) + matmul_nt(low[rows, :], right_side[...])
        whole = both[:, :HD] + both[:, HD:]
        part[2 * c] = whole[:TOK]
        part[2 * c + 1] = whole[TOK:]

    def back_y(part, full_in, half_in, send, recv):
        copies = {}
        for d, (sign, where) in enumerate(((-1, down), (1, up))):
            rows = pl.ds(d * HALF, HALF)
            for j, n in enumerate((4, 3, 2, 1)):
                src = part.at[PLACE[(-sign * n) % NY]]
                if j == 0:
                    copies[j, d] = remote(src.at[rows], half_in.at[d], send.at[d], recv.at[d], where)
                else:
                    at = 2 * j + d
                    copies[j, d] = remote(src, full_in.at[2 * (j - 1) + d], send.at[at], recv.at[at], where)
        return copies

    def join_y(copies, j, part, full_in, half_in):
        for d, sign in enumerate((-1, 1)):
            place = PLACE[(-sign * (4 - j)) % NY]
            copies[j - 1, d].wait_recv()
            if j == 1:
                rows = pl.ds(d * HALF, HALF)
                part[place, rows, :] = part[place, rows, :] + half_in[d]
            else:
                part[place] = part[place] + full_in[2 * (j - 2) + d]
            if j < 4:
                copies[j, d].start()

    def back_x(part, full_in, half_in, send, recv):
        copies = {}
        for d, where in enumerate((right, left)):
            rows = pl.ds(d * HALF, HALF)
            near = 3 if d == 0 else 1
            copies[0, d] = remote(part.at[2, rows], half_in.at[d], send.at[d], recv.at[d], where)
            copies[1, d] = remote(part.at[near], full_in.at[d], send.at[2 + d], recv.at[2 + d], where)
        return copies

    def join_x(copies, part, half_in):
        for d in range(2):
            near = 3 if d == 0 else 1
            rows = pl.ds(d * HALF, HALF)
            copies[0, d].wait_recv()
            part[near, rows, :] = part[near, rows, :] + half_in[d]
            copies[1, d].start()

    dv_go = back_y(dv_part, dv_in, dv_half, dvy_s, dvy_r)
    dk_go = back_y(dk_part, dk_in, dk_half, dky_s, dky_r)
    o_go = back_x(o_part, o_in, o_half, ox_s, ox_r)
    dq_go = back_x(dq_part, dq_in, dq_half, dqx_s, dqx_r)
    everything += [*st_go, *dv_go.values(), *dk_go.values(), *o_go.values(), *dq_go.values()]

    key_side(3, p_hi, p_lo, gf, dv_part)
    for d in range(2):
        dv_go[0, d].start()

    ready_value(5)
    ready_value(6)
    weigh_chunk(2)
    pass_on(v_go, 4, 3)
    ready_value(7)
    weigh_chunk(3)
    dots[0] = jnp.sum(dot8[...], axis=0, keepdims=True) * scaled[...]
    rd_go = [
        remote(dots.at[0], dots.at[n + 1], rd_s.at[n], rd_r.at[n], peers[n]) for n in range(NX - 1)
    ]
    everything += rd_go
    for copy in rd_go:
        copy.start()

    key_side(2, p_hi, p_lo, gf, dv_part)
    join_y(dv_go, 1, dv_part, dv_in, dv_half)

    def query_side(s, sides, high, low, part, scale):
        cols = pl.ds(s * QCOLS, QCOLS)
        both = matmul(sides[...], high[:, cols]) + matmul(sides[...], low[:, cols])
        part[s] = (both[:HD] + both[HD:]) * (scaled[:, cols] * scale)

    query_side(2, vt, p_hi, p_lo, o_part, 1.0)
    for d in range(2):
        o_go[0, d].start()
    key_side(1, p_hi, p_lo, gf, dv_part)
    join_y(dv_go, 2, dv_part, dv_in, dv_half)
    query_side(1, vt, p_hi, p_lo, o_part, 1.0)
    query_side(3, vt, p_hi, p_lo, o_part, 1.0)
    join_x(o_go, o_part, o_half)
    key_side(0, p_hi, p_lo, gf, dv_part)
    join_y(dv_go, 3, dv_part, dv_in, dv_half)

    for copy in rd_go:
        copy.wait_recv()
    row_dot = dots[0]
    for n in range(NX - 1):
        row_dot = row_dot + aligned(dots[n + 1], n)

    def grad_chunk(c):
        rows = pl.ds(c * CHUNK, CHUNK)
        for s in range(NX):
            cols = pl.ds(s * QCOLS, QCOLS)
            value = scores[rows, cols] * (gw[rows, cols] - row_dot[:, s * QCOLS:(s + 1) * QCOLS])
            high, low = split2(value)
            t_hi[rows, cols] = high
            t_lo[rows, cols] = low

    grad_chunk(3)
    key_side(3, t_hi, t_lo, qf, dk_part)
    for d in range(2):
        dk_go[0, d].start()
    grad_chunk(2)
    key_side(2, t_hi, t_lo, qf, dk_part)
    join_y(dk_go, 1, dk_part, dk_in, dk_half)
    grad_chunk(1)
    grad_chunk(0)
    query_side(2, kt, t_hi, t_lo, dq_part, SCALE)
    for d in range(2):
        dq_go[0, d].start()
    key_side(1, t_hi, t_lo, qf, dk_part)
    join_y(dk_go, 2, dk_part, dk_in, dk_half)
    query_side(1, kt, t_hi, t_lo, dq_part, SCALE)
    query_side(3, kt, t_hi, t_lo, dq_part, SCALE)
    join_x(dq_go, dq_part, dq_half)
    key_side(0, t_hi, t_lo, qf, dk_part)
    join_y(dk_go, 3, dk_part, dk_in, dk_half)
    query_side(0, vt, p_hi, p_lo, o_part, 1.0)
    query_side(0, kt, t_hi, t_lo, dq_part, SCALE)

    def finish_x(copies, part, full_in, out):
        for d in range(2):
            copies[1, d].wait_recv()
        whole = part[0] + full_in[0] + full_in[1]
        for h in range(HEADS):
            out[0, :, h * HD:(h + 1) * HD] = whole[:, h * TOK:(h + 1) * TOK].T

    finish_x(o_go, o_part, o_in, o_out)
    join_y(dv_go, 4, dv_part, dv_in, dv_half)
    dv_out[0] = dv_part[0]
    finish_x(dq_go, dq_part, dq_in, dq_out)
    join_y(dk_go, 4, dk_part, dk_in, dk_half)
    dk_out[0] = dk_part[0] * LN2
    for copy in everything:
        copy.wait_send()


def body(queries, key_rows, value_rows, cotangent, block_order):
    def vmem(*shape, dtype=F32):
        return pltpu.VMEM(shape, dtype)

    dma = lambda n: pltpu.SemaphoreType.DMA((n,))
    in_vmem = pl.BlockSpec(memory_space=pltpu.VMEM)
    anywhere = pl.BlockSpec(memory_space=pl.ANY)
    wide = jax.ShapeDtypeStruct((1, TOK, HEADS * HD), F32)
    narrow = jax.ShapeDtypeStruct((1, TOK, HD), F32)
    return pl.pallas_call(
        kernel,
        out_shape=(wide, wide, narrow, narrow),
        in_specs=[pl.BlockSpec(memory_space=pltpu.SMEM)] + [anywhere] * 4,
        out_specs=[in_vmem] * 4,
        scratch_shapes=[
            vmem(TOK, HEADS * HD), vmem(TOK, HEADS * HD),
            vmem(NX, HD, QCOLS), vmem(NX, HD, QCOLS),
            vmem(NY, TOK, HD), vmem(NY, TOK, HD),
            vmem(6 * HD, ALLQ, dtype=BF16), vmem(3 * HD, ALLQ, dtype=BF16),
            vmem(ALLK, 6 * HD, dtype=BF16), vmem(ALLK, 3 * HD, dtype=BF16),
            vmem(2 * HD, ALLK, dtype=BF16), vmem(2 * HD, ALLK, dtype=BF16),
            vmem(2 * HD, ALLQ, dtype=BF16), vmem(2 * HD, ALLQ, dtype=BF16),
            vmem(ALLK, ALLQ), vmem(ALLK, ALLQ),
            vmem(ALLK, ALLQ, dtype=BF16), vmem(ALLK, ALLQ, dtype=BF16),
            vmem(ALLK, ALLQ, dtype=BF16), vmem(ALLK, ALLQ, dtype=BF16),
            vmem(8, ALLQ), vmem(8, ALLQ), vmem(8, ALLQ),
            vmem(NX, 2, ALLQ), vmem(NX, 1, ALLQ), vmem(1, ALLQ),
            vmem(NY, TOK, HD), vmem(NY, TOK, HD),
            vmem(NX, HD, QCOLS), vmem(NX, HD, QCOLS),
            vmem(6, TOK, HD), vmem(2, HALF, HD), vmem(6, TOK, HD), vmem(2, HALF, HD),
            vmem(2, HD, QCOLS), vmem(2, HALF, QCOLS), vmem(2, HD, QCOLS), vmem(2, HALF, QCOLS),
            dma(4),
            dma(4), dma(4), dma(4), dma(4), dma(8), dma(8), dma(8), dma(8),
            dma(3), dma(3), dma(3), dma(3),
            dma(8), dma(8), dma(8), dma(8), dma(4), dma(4), dma(4), dma(4),
        ],
        compiler_params=pltpu.CompilerParams(
            collective_id=0, has_side_effects=True, vmem_limit_bytes=52 * 1024 * 1024
        ),
    )(block_order, queries, key_rows, value_rows, cotangent)


def solution(mesh):
    spread = P("outer", "inner", None)
    return jax.shard_map(
        body,
        mesh=mesh,
        in_specs=(spread, spread, spread, spread, P()),
        out_specs=(spread, spread, spread, spread),
        check_vma=False,
    )
```

```python
import jax
import jax.numpy as jnp
from jax import lax
from jax.experimental import pallas as pl
from jax.experimental.pallas import tpu as pltpu
from jax.sharding import PartitionSpec as P

HD = 128
HEADS = 2
GROUPS = 4
TOK = 128
NX = 4
NY = 8
QCOLS = HEADS * TOK
ALLQ = NX * QCOLS
ALLK = NY * TOK
HALF = TOK // 2
SCALE = HD ** (-0.5)
LOG2E = 1.4426950408889634
LN2 = 0.6931471805599453
FAR = -1e30
MESH = pl.DeviceIdType.MESH
F32 = jnp.float32
BF16 = jnp.bfloat16

AT = (2, 6, 1, 7, 3, 5, 0, 4)
PLACE = tuple(AT.index(r) for r in range(NY))
OWN = PLACE[0]
CHUNK = 2 * TOK


def split2(value):
    high = value.astype(BF16)
    return high, (value - high.astype(F32)).astype(BF16)


def split3(value):
    high = value.astype(BF16)
    rest = value - high.astype(F32)
    mid = rest.astype(BF16)
    return high, mid, (rest - mid.astype(F32)).astype(BF16)


def matmul(left, right):
    return jnp.dot(left, right, preferred_element_type=F32)


def matmul_nt(left, right):
    return lax.dot_general(left, right, (((1,), (1,)), ((), ())), preferred_element_type=F32)


def fold_rows(value, combine):
    return combine(value.reshape(value.shape[0] // 8, 8, value.shape[1]), axis=0)


def kernel(
    order_hbm, q_hbm, k_hbm, v_hbm, g_hbm, o_out, dq_out, dk_out, dv_out,
    order, q_own, g_own, q_t, g_t, keys, vals, qs, gs, kp, vp, kt, vt, qf, gf,
    scores, gw, p_hi, p_lo, t_hi, t_lo, max8, sum8, dot8, stats, dots, scaled,
    dv_part, dk_part, o_part, dq_part, dv_in, dv_half, dk_in, dk_half, o_in, dq_in,
    local_sem, qx_s, qx_r, gx_s, gx_r, ky_s, ky_r, vy_s, vy_r, st_s, st_r, rd_s, rd_r,
    dvy_s, dvy_r, dky_s, dky_r, ox_s, ox_r, dqx_s, dqx_r,
):
    seqs = lax.axis_size("outer") // GROUPS
    outer = lax.axis_index("outer")
    inner = lax.axis_index("inner")
    seq = lax.rem(outer, seqs)
    x = lax.rem(inner, NX)
    y = (inner // NX) * GROUPS + outer // seqs

    def device(at_x, at_y):
        return (lax.rem(at_y, GROUPS) * seqs + seq, (at_y // GROUPS) * NX + at_x)

    def along_x(step):
        return device(lax.rem(x + step + NX, NX), y)

    def along_y(step):
        return device(x, lax.rem(y + step + NY, NY))

    def position(at_x, at_y):
        return order[lax.rem(at_y, GROUPS) * (NX * NY // GROUPS) + (at_y // GROUPS) * NX + at_x]

    def remote(src, dst, send, recv, where):
        return pltpu.make_async_remote_copy(
            src_ref=src, dst_ref=dst, send_sem=send, recv_sem=recv, device_id=where, device_id_type=MESH
        )

    up, down, up2, down2 = along_y(1), along_y(-1), along_y(2), along_y(-2)
    right, left, across = along_x(1), along_x(-1), along_x(2)
    peers = (right, across, left)

    loads = [
        pltpu.make_async_copy(q_hbm.at[0], q_own, local_sem.at[0]),
        pltpu.make_async_copy(g_hbm.at[0], g_own, local_sem.at[1]),
        pltpu.make_async_copy(k_hbm.at[0], keys.at[OWN], local_sem.at[2]),
        pltpu.make_async_copy(v_hbm.at[0], vals.at[OWN], local_sem.at[3]),
        pltpu.make_async_copy(order_hbm, order, local_sem.at[4]),
    ]
    for load in loads:
        load.start()
    barrier = pltpu.get_barrier_semaphore()
    for peer in (up, down, up2, down2, right, left, across):
        pl.semaphore_signal(barrier, inc=1, device_id=peer, device_id_type=MESH)
    pl.semaphore_wait(barrier, 7)

    ways = ((1, up, up2), (-1, down, down2))

    def gather_y(own, buf, send, recv, by_two):
        copies = {}
        for d, (sign, near, far) in enumerate(ways):
            at = [buf.at[PLACE[(sign * n) % NY]] for n in range(5)]
            rows = pl.ds(d * HALF, HALF)
            copies[d, 1] = remote(own, at[1], send.at[4 * d], recv.at[4 * d], near)
            if by_two:
                copies[d, 2] = remote(own, at[2], send.at[4 * d + 1], recv.at[4 * d + 1], far)
            else:
                copies[d, 2] = remote(at[1], at[2], send.at[4 * d + 1], recv.at[4 * d + 1], near)
            copies[d, 3] = remote(at[2], at[3], send.at[4 * d + 2], recv.at[4 * d + 2], near)
            copies[d, 4] = remote(at[2].at[rows], at[4].at[rows], send.at[4 * d + 3], recv.at[4 * d + 3], far)
        return copies

    def gather_x(buf, send, recv):
        return [
            remote(buf.at[0], buf.at[n + 1], send.at[n], recv.at[n], peers[n]) for n in range(NX - 1)
        ]

    k_go, v_go = gather_y(k_hbm.at[0], keys, ky_s, ky_r, True), gather_y(v_hbm.at[0], vals, vy_s, vy_r, False)
    q_go, g_go = gather_x(q_t, qx_s, qx_r), gather_x(g_t, gx_s, gx_r)
    gathered = [*k_go.values(), *v_go.values(), *q_go, *g_go]
    everything = []

    def start(copies, n):
        for d in range(2):
            copies[d, n].start()

    def arrived(copies, n):
        for d in range(2):
            copies[d, n].wait_recv()

    def ready_query(s):
        cols = pl.ds(s * QCOLS, QCOLS)
        q0, q1, q2 = split3(q_t[s])
        for n, piece in enumerate((q0, q1, q0, q1, q0, q2)):
            qs[n * HD:(n + 1) * HD, cols] = piece

    def ready_cotangent(s):
        cols = pl.ds(s * QCOLS, QCOLS)
        g0, g1 = split2(g_t[s])
        for n, piece in enumerate((g0, g1, g0)):
            gs[n * HD:(n + 1) * HD, cols] = piece

    def ready_key(place):
        rows = pl.ds(place * TOK, TOK)
        k0, k1, k2 = split3(keys[place])
        for n, piece in enumerate((k0, k0, k1, k1, k2, k0)):
            kp[rows, n * HD:(n + 1) * HD] = piece
        high, low = split2(keys[place].T)
        kt[0:HD, rows] = high
        kt[HD:2 * HD, rows] = low

    def ready_value(place):
        rows = pl.ds(place * TOK, TOK)
        v0, v1 = split2(vals[place])
        for n, piece in enumerate((v0, v0, v1)):
            vp[rows, n * HD:(n + 1) * HD] = piece
        high, low = split2(vals[place].T)
        vt[0:HD, rows] = high
        vt[HD:2 * HD, rows] = low

    def score_chunk(c):
        rows = pl.ds(c * CHUNK, CHUNK)
        for s in range(NX):
            cols = pl.ds(s * QCOLS, QCOLS)
            query_at = position(lax.rem(x - s + NX, NX), y)
            tile = matmul(kp[rows, :], qs[:, cols])
            parts = []
            for n in range(2):
                r = AT[2 * c + n]
                part = tile[n * TOK:(n + 1) * TOK]
                if r == 0 and s == 0:
                    key_at = lax.broadcasted_iota(jnp.int32, (TOK, QCOLS), 0)
                    token = lax.rem(lax.broadcasted_iota(jnp.int32, (TOK, QCOLS), 1), TOK)
                    part = jnp.where(key_at <= token, part, FAR)
                else:
                    seen = position(x, lax.rem(y - r + NY, NY)) <= query_at
                    part = part + jnp.where(seen, 0.0, FAR).astype(F32)
                parts.append(part)
            for n, part in enumerate(parts):
                scores[c * CHUNK + n * TOK:c * CHUNK + (n + 1) * TOK, cols] = part
            top = jnp.maximum(fold_rows(parts[0], jnp.max), fold_rows(parts[1], jnp.max))
            max8[:, cols] = top if c == 0 else jnp.maximum(max8[:, cols], top)

    start(k_go, 2)
    start(k_go, 1)
    loads[0].wait()
    for h in range(HEADS):
        q_t[0, :, h * TOK:(h + 1) * TOK] = q_own[:, h * HD:(h + 1) * HD].T * (SCALE * LOG2E)
    for n in (1, 0, 2):
        q_go[n].start()
    start(v_go, 1)
    loads[1].wait()
    for h in range(HEADS):
        g_t[0, :, h * TOK:(h + 1) * TOK] = g_own[:, h * HD:(h + 1) * HD].T
    for n in (1, 0, 2):
        g_go[n].start()
    for load in loads[2:]:
        load.wait()
    ready_query(0)
    ready_key(OWN)
    ready_cotangent(0)
    ready_value(OWN)

    arrived(k_go, 2)
    start(k_go, 4)
    start(k_go, 3)
    ready_key(0)
    ready_key(1)
    arrived(k_go, 1)
    ready_key(2)
    ready_key(3)
    q_go[0].wait_recv()
    ready_query(1)
    q_go[2].wait_recv()
    ready_query(3)
    arrived(v_go, 1)
    start(v_go, 2)
    q_go[1].wait_recv()
    ready_query(2)
    score_chunk(0)
    score_chunk(1)
    arrived(k_go, 3)
    ready_key(4)
    ready_key(5)
    score_chunk(2)
    arrived(k_go, 4)
    ready_key(7)
    score_chunk(3)
    arrived(v_go, 2)
    start(v_go, 4)
    start(v_go, 3)

    top = jnp.max(max8[...], axis=0, keepdims=True)
    def soft_chunk(c):
        rows = pl.ds(c * CHUNK, CHUNK)
        for s in range(NX):
            cols = pl.ds(s * QCOLS, QCOLS)
            weight = jnp.exp2(scores[rows, cols] - top[:, s * QCOLS:(s + 1) * QCOLS])
            scores[rows, cols] = weight
            high, low = split2(weight)
            p_hi[rows, cols] = high
            p_lo[rows, cols] = low
            part = fold_rows(weight, jnp.sum)
            sum8[:, cols] = part if c == 0 else sum8[:, cols] + part

    for c in range(NY // 2):
        soft_chunk(c)
    stats[0, 0:1, :] = top
    stats[0, 1:2, :] = jnp.sum(sum8[...], axis=0, keepdims=True)
    st_go = [
        remote(stats.at[0], stats.at[n + 1], st_s.at[n], st_r.at[n], peers[n]) for n in range(NX - 1)
    ]
    for copy in st_go:
        copy.start()

    for place in range(4):
        ready_value(place)
    for n in range(NX - 1):
        g_go[n].wait_recv()
        ready_cotangent(n + 1)

    def weigh_chunk(c):
        rows = pl.ds(c * CHUNK, CHUNK)
        for s in range(NX):
            cols = pl.ds(s * QCOLS, QCOLS)
            tile = matmul(vp[rows, :], gs[:, cols])
            gw[rows, cols] = tile
            part = fold_rows(tile * scores[rows, cols], jnp.sum)
            dot8[:, cols] = part if c == 0 else dot8[:, cols] + part

    weigh_chunk(0)
    weigh_chunk(1)

    def aligned(row, n):
        cut = ALLQ - (n + 1) * QCOLS
        return jnp.concatenate([row[:, cut:], row[:, :cut]], axis=1)

    for copy in st_go:
        copy.wait_recv()
    tops = [aligned(stats[n + 1, 0:1, :], n) for n in range(NX - 1)]
    whole_top = jnp.maximum(jnp.maximum(top, tops[0]), jnp.maximum(tops[1], tops[2]))
    own_factor = jnp.exp2(top - whole_top)
    total = own_factor * stats[0, 1:2, :]
    for n in range(NX - 1):
        total = total + jnp.exp2(tops[n] - whole_top) * aligned(stats[n + 1, 1:2, :], n)
    factor = own_factor / total
    scaled[...] = factor

    for s in range(NX):
        cols = pl.ds(s * QCOLS, QCOLS)
        row = scaled[:, cols]
        high, low = split2(g_t[s] * row)
        gf[0:HD, cols] = high
        gf[HD:2 * HD, cols] = low
        high, low = split2(q_t[s] * row)
        qf[0:HD, cols] = high
        qf[HD:2 * HD, cols] = low

    def key_side(c, high, low, right_side, part):
        rows = pl.ds(c * CHUNK, CHUNK)
        both = matmul_nt(high[rows, :], right_side[...]) + matmul_nt(low[rows, :], right_side[...])
        whole = both[:, :HD] + both[:, HD:]
        part[2 * c] = whole[:TOK]
        part[2 * c + 1] = whole[TOK:]

    def back_y(part, whole_in, half_in, send, recv, by_two):
        copies = {}
        for d, (sign, near, far) in enumerate(ways):
            at = [part.at[PLACE[(-sign * n) % NY]] for n in range(5)]
            rows = pl.ds(d * HALF, HALF)
            sems = [(send.at[4 * d + n], recv.at[4 * d + n]) for n in range(4)]
            copies[d, 4] = remote(at[4].at[rows], half_in.at[d], *sems[3], far)
            copies[d, 3] = remote(at[3], whole_in.at[d], *sems[2], near)
            copies[d, 2] = remote(at[2], whole_in.at[2 + d], *sems[1], far if by_two else near)
            copies[d, 1] = remote(at[1], whole_in.at[4 + d], *sems[0], near)
        return copies

    def join_far(copies, part, whole_in, half_in):
        for d, (sign, _, _) in enumerate(ways):
            place = PLACE[(-sign * 2) % NY]
            copies[d, 3].wait_recv()
            part[place] = part[place] + whole_in[d]
            copies[d, 4].wait_recv()
            rows = pl.ds(d * HALF, HALF)
            part[place, rows, :] = part[place, rows, :] + half_in[d]
            copies[d, 2].start()

    def join_near(copies, part, whole_in):
        for d, (sign, _, _) in enumerate(ways):
            place = PLACE[(-sign) % NY]
            copies[d, 2].wait_recv()
            part[place] = part[place] + whole_in[2 + d]
            copies[d, 1].start()

    def back_x(part, into, send, recv):
        return [
            remote(part.at[NX - 1 - n], into.at[n], send.at[n], recv.at[n], peers[n]) for n in range(NX - 1)
        ]

    dv_go = back_y(dv_part, dv_in, dv_half, dvy_s, dvy_r, False)
    dk_go = back_y(dk_part, dk_in, dk_half, dky_s, dky_r, True)
    o_go = back_x(o_part, o_in, ox_s, ox_r)
    dq_go = back_x(dq_part, dq_in, dqx_s, dqx_r)
    everything += [*dv_go.values(), *dk_go.values(), *o_go, *dq_go]

    key_side(2, p_hi, p_lo, gf, dv_part)
    start(dv_go, 3)
    key_side(3, p_hi, p_lo, gf, dv_part)
    start(dv_go, 4)
    key_side(0, p_hi, p_lo, gf, dv_part)

    arrived(v_go, 3)
    ready_value(4)
    ready_value(5)
    weigh_chunk(2)
    arrived(v_go, 4)
    ready_value(7)
    weigh_chunk(3)
    dots[0] = jnp.sum(dot8[...], axis=0, keepdims=True) * scaled[...]
    rd_go = [
        remote(dots.at[0], dots.at[n + 1], rd_s.at[n], rd_r.at[n], peers[n]) for n in range(NX - 1)
    ]
    everything += rd_go
    for copy in rd_go:
        copy.start()
    key_side(1, p_hi, p_lo, gf, dv_part)

    def query_side(s, sides, high, low, part, scale):
        cols = pl.ds(s * QCOLS, QCOLS)
        both = matmul(sides[...], high[:, cols]) + matmul(sides[...], low[:, cols])
        part[s] = (both[:HD] + both[HD:]) * (scaled[:, cols] * scale)

    for n in (1, 0, 2):
        query_side(NX - 1 - n, vt, p_hi, p_lo, o_part, 1.0)
        o_go[n].start()
    query_side(0, vt, p_hi, p_lo, o_part, 1.0)

    for copy in [*gathered, *st_go]:
        copy.wait_send()
    for copy in rd_go:
        copy.wait_recv()
    row_dot = dots[0]
    for n in range(NX - 1):
        row_dot = row_dot + aligned(dots[n + 1], n)

    def grad_chunk(c):
        rows = pl.ds(c * CHUNK, CHUNK)
        for s in range(NX):
            cols = pl.ds(s * QCOLS, QCOLS)
            value = scores[rows, cols] * (gw[rows, cols] - row_dot[:, s * QCOLS:(s + 1) * QCOLS])
            high, low = split2(value)
            t_hi[rows, cols] = high
            t_lo[rows, cols] = low

    grad_chunk(2)
    key_side(2, t_hi, t_lo, qf, dk_part)
    start(dk_go, 3)
    grad_chunk(3)
    key_side(3, t_hi, t_lo, qf, dk_part)
    start(dk_go, 4)
    join_far(dv_go, dv_part, dv_in, dv_half)
    grad_chunk(0)
    key_side(0, t_hi, t_lo, qf, dk_part)
    grad_chunk(1)
    for n in (1, 0, 2):
        query_side(NX - 1 - n, kt, t_hi, t_lo, dq_part, SCALE)
        dq_go[n].start()
    key_side(1, t_hi, t_lo, qf, dk_part)
    start(dk_go, 1)
    join_far(dk_go, dk_part, dk_in, dk_half)
    join_near(dv_go, dv_part, dv_in)
    query_side(0, kt, t_hi, t_lo, dq_part, SCALE)

    def finish_x(copies, part, full_in, out):
        for copy in copies:
            copy.wait_recv()
        whole = (part[0] + full_in[0]) + (full_in[1] + full_in[2])
        for h in range(HEADS):
            out[0, :, h * HD:(h + 1) * HD] = whole[:, h * TOK:(h + 1) * TOK].T

    finish_x(o_go, o_part, o_in, o_out)
    arrived(dv_go, 1)
    dv_out[0] = dv_part[OWN] + (dv_in[4] + dv_in[5])
    finish_x(dq_go, dq_part, dq_in, dq_out)
    arrived(dk_go, 2)
    arrived(dk_go, 1)
    dk_out[0] = (dk_part[OWN] + ((dk_in[2] + dk_in[3]) + (dk_in[4] + dk_in[5]))) * LN2
    for copy in everything:
        copy.wait_send()


def store(*refs):
    sources, targets, sems = refs[:4], refs[4:8], refs[8]
    copies = [pltpu.make_async_copy(a, b, sems.at[n]) for n, (a, b) in enumerate(zip(sources, targets))]
    for copy in copies:
        copy.start()
    for copy in copies:
        copy.wait()


def body(queries, key_rows, value_rows, cotangent, block_order):
    def vmem(*shape, dtype=F32):
        return pltpu.VMEM(shape, dtype)

    dma = lambda n: pltpu.SemaphoreType.DMA((n,))
    in_vmem = pl.BlockSpec(memory_space=pltpu.VMEM)
    in_hbm = pl.BlockSpec(memory_space=pltpu.HBM)
    wide = jax.ShapeDtypeStruct((1, TOK, HEADS * HD), F32)
    narrow = jax.ShapeDtypeStruct((1, TOK, HD), F32)
    shapes = (wide, wide, narrow, narrow)
    results = pl.pallas_call(
        kernel,
        out_shape=shapes,
        in_specs=[in_hbm] * 5,
        out_specs=[in_vmem] * 4,
        scratch_shapes=[
            pltpu.SMEM((NX * NY,), jnp.int32), vmem(TOK, HEADS * HD), vmem(TOK, HEADS * HD),
            vmem(NX, HD, QCOLS), vmem(NX, HD, QCOLS),
            vmem(NY, TOK, HD), vmem(NY, TOK, HD),
            vmem(6 * HD, ALLQ, dtype=BF16), vmem(3 * HD, ALLQ, dtype=BF16),
            vmem(ALLK, 6 * HD, dtype=BF16), vmem(ALLK, 3 * HD, dtype=BF16),
            vmem(2 * HD, ALLK, dtype=BF16), vmem(2 * HD, ALLK, dtype=BF16),
            vmem(2 * HD, ALLQ, dtype=BF16), vmem(2 * HD, ALLQ, dtype=BF16),
            vmem(ALLK, ALLQ), vmem(ALLK, ALLQ),
            vmem(ALLK, ALLQ, dtype=BF16), vmem(ALLK, ALLQ, dtype=BF16),
            vmem(ALLK, ALLQ, dtype=BF16), vmem(ALLK, ALLQ, dtype=BF16),
            vmem(8, ALLQ), vmem(8, ALLQ), vmem(8, ALLQ),
            vmem(NX, 2, ALLQ), vmem(NX, 1, ALLQ), vmem(1, ALLQ),
            vmem(NY, TOK, HD), vmem(NY, TOK, HD),
            vmem(NX, HD, QCOLS), vmem(NX, HD, QCOLS),
            vmem(6, TOK, HD), vmem(2, HALF, HD), vmem(6, TOK, HD), vmem(2, HALF, HD),
            vmem(3, HD, QCOLS), vmem(3, HD, QCOLS),
            dma(5),
            dma(3), dma(3), dma(3), dma(3), dma(8), dma(8), dma(8), dma(8),
            dma(3), dma(3), dma(3), dma(3),
            dma(8), dma(8), dma(8), dma(8), dma(3), dma(3), dma(3), dma(3),
        ],
        compiler_params=pltpu.CompilerParams(
            collective_id=0, has_side_effects=True, vmem_limit_bytes=44 * 1024 * 1024
        ),
    )(*(pltpu.with_memory_space_constraint(a, pltpu.HBM) for a in (block_order, queries, key_rows, value_rows, cotangent)))
    return pl.pallas_call(
        store,
        out_shape=shapes,
        in_specs=[in_vmem] * 4,
        out_specs=[in_hbm] * 4,
        scratch_shapes=[dma(4)],
    )(*results)


def solution(mesh):
    spread = P("outer", "inner", None)
    return jax.shard_map(
        body,
        mesh=mesh,
        in_specs=(spread, spread, spread, spread, P()),
        out_specs=(spread, spread, spread, spread),
        check_vma=False,
    )
```

```python
import jax
import jax.numpy as jnp
from jax import lax
from jax.experimental import pallas as pl
from jax.experimental.pallas import tpu as pltpu
from jax.sharding import PartitionSpec as P

HD = 128
HEADS = 2
GROUPS = 4
TOK = 128
NX = 4
NY = 8
QCOLS = HEADS * TOK
ALLQ = NX * QCOLS
ALLK = NY * TOK
HALF = TOK // 2
SCALE = HD ** (-0.5)
LOG2E = 1.4426950408889634
LN2 = 0.6931471805599453
FAR = -1e30
MESH = pl.DeviceIdType.MESH
F32 = jnp.float32
BF16 = jnp.bfloat16

AT = (2, 6, 1, 7, 3, 5, 0, 4)
PLACE = tuple(AT.index(r) for r in range(NY))
OWN = PLACE[0]
CHUNK = 2 * TOK


def split2(value):
    high = value.astype(BF16)
    return high, (value - high.astype(F32)).astype(BF16)


def split3(value):
    high = value.astype(BF16)
    rest = value - high.astype(F32)
    mid = rest.astype(BF16)
    return high, mid, (rest - mid.astype(F32)).astype(BF16)


def matmul(left, right):
    return jnp.dot(left, right, preferred_element_type=F32)


def matmul_nt(left, right):
    return lax.dot_general(left, right, (((1,), (1,)), ((), ())), preferred_element_type=F32)


def fold_rows(value, combine):
    return combine(value.reshape(value.shape[0] // 8, 8, value.shape[1]), axis=0)


def kernel(
    order_hbm, q_hbm, k_hbm, v_hbm, g_hbm, o_out, dq_out, dk_out, dv_out,
    order, q_own, g_own, q_t, g_t, keys, vals, qs, gs, kp, vp, kt, vt, qf, gf,
    scores, gw, p_hi, p_lo, t_hi, t_lo, max8, sum8, dot8, stats, dots, scaled,
    dv_part, dk_part, o_part, dq_part, dv_in, dv_half, dk_in, dk_half, o_in, dq_in,
    local_sem, qx_s, qx_r, gx_s, gx_r, ky_s, ky_r, vy_s, vy_r, st_s, st_r, rd_s, rd_r,
    dvy_s, dvy_r, dky_s, dky_r, ox_s, ox_r, dqx_s, dqx_r,
):
    seqs = lax.axis_size("outer") // GROUPS
    outer = lax.axis_index("outer")
    inner = lax.axis_index("inner")
    seq = lax.rem(outer, seqs)
    x = lax.rem(inner, NX)
    y = (inner // NX) * GROUPS + outer // seqs

    def device(at_x, at_y):
        return (lax.rem(at_y, GROUPS) * seqs + seq, (at_y // GROUPS) * NX + at_x)

    def along_x(step):
        return device(lax.rem(x + step + NX, NX), y)

    def along_y(step):
        return device(x, lax.rem(y + step + NY, NY))

    def position(at_x, at_y):
        return order[lax.rem(at_y, GROUPS) * (NX * NY // GROUPS) + (at_y // GROUPS) * NX + at_x]

    def remote(src, dst, send, recv, where):
        return pltpu.make_async_remote_copy(
            src_ref=src, dst_ref=dst, send_sem=send, recv_sem=recv, device_id=where, device_id_type=MESH
        )

    up, down, up2, down2 = along_y(1), along_y(-1), along_y(2), along_y(-2)
    right, left, across = along_x(1), along_x(-1), along_x(2)
    peers = (right, across, left)

    loads = [
        pltpu.make_async_copy(q_hbm.at[0], q_own, local_sem.at[0]),
        pltpu.make_async_copy(g_hbm.at[0], g_own, local_sem.at[1]),
        pltpu.make_async_copy(k_hbm.at[0], keys.at[OWN], local_sem.at[2]),
        pltpu.make_async_copy(v_hbm.at[0], vals.at[OWN], local_sem.at[3]),
        pltpu.make_async_copy(order_hbm, order, local_sem.at[4]),
    ]
    for load in loads:
        load.start()
    barrier = pltpu.get_barrier_semaphore()
    for peer in (up, down, up2, down2, right, left, across):
        pl.semaphore_signal(barrier, inc=1, device_id=peer, device_id_type=MESH)
    pl.semaphore_wait(barrier, 7)

    ways = ((1, up, up2), (-1, down, down2))

    def gather_y(own, buf, send, recv, by_two):
        copies = {}
        for d, (sign, near, far) in enumerate(ways):
            at = [buf.at[PLACE[(sign * n) % NY]] for n in range(5)]
            rows = pl.ds(d * HALF, HALF)
            copies[d, 1] = remote(own, at[1], send.at[4 * d], recv.at[4 * d], near)
            if by_two:
                copies[d, 2] = remote(own, at[2], send.at[4 * d + 1], recv.at[4 * d + 1], far)
            else:
                copies[d, 2] = remote(at[1], at[2], send.at[4 * d + 1], recv.at[4 * d + 1], near)
            copies[d, 3] = remote(at[2], at[3], send.at[4 * d + 2], recv.at[4 * d + 2], near)
            copies[d, 4] = remote(at[2].at[rows], at[4].at[rows], send.at[4 * d + 3], recv.at[4 * d + 3], far)
        return copies

    def gather_x(buf, send, recv):
        return [
            remote(buf.at[0], buf.at[n + 1], send.at[n], recv.at[n], peers[n]) for n in range(NX - 1)
        ]

    k_go, v_go = gather_y(k_hbm.at[0], keys, ky_s, ky_r, True), gather_y(v_hbm.at[0], vals, vy_s, vy_r, False)
    q_go, g_go = gather_x(q_t, qx_s, qx_r), gather_x(g_t, gx_s, gx_r)
    gathered = [*k_go.values(), *v_go.values(), *q_go, *g_go]
    everything = []

    def start(copies, n):
        for d in range(2):
            copies[d, n].start()

    def arrived(copies, n):
        for d in range(2):
            copies[d, n].wait_recv()

    def ready_query(s):
        cols = pl.ds(s * QCOLS, QCOLS)
        q0, q1, q2 = split3(q_t[s])
        for n, piece in enumerate((q0, q1, q0, q1, q0, q2)):
            qs[n * HD:(n + 1) * HD, cols] = piece

    def ready_cotangent(s):
        cols = pl.ds(s * QCOLS, QCOLS)
        g0, g1 = split2(g_t[s])
        for n, piece in enumerate((g0, g1, g0)):
            gs[n * HD:(n + 1) * HD, cols] = piece

    def ready_key(place):
        rows = pl.ds(place * TOK, TOK)
        k0, k1, k2 = split3(keys[place])
        for n, piece in enumerate((k0, k0, k1, k1, k2, k0)):
            kp[rows, n * HD:(n + 1) * HD] = piece
        high, low = split2(keys[place].T)
        kt[0:HD, rows] = high
        kt[HD:2 * HD, rows] = low

    def ready_value(place):
        rows = pl.ds(place * TOK, TOK)
        v0, v1 = split2(vals[place])
        for n, piece in enumerate((v0, v0, v1)):
            vp[rows, n * HD:(n + 1) * HD] = piece
        high, low = split2(vals[place].T)
        vt[0:HD, rows] = high
        vt[HD:2 * HD, rows] = low

    def score_chunk(c):
        rows = pl.ds(c * CHUNK, CHUNK)
        for s in range(NX):
            cols = pl.ds(s * QCOLS, QCOLS)
            query_at = position(lax.rem(x - s + NX, NX), y)
            tile = matmul(kp[rows, :], qs[:, cols])
            parts = []
            for n in range(2):
                r = AT[2 * c + n]
                part = tile[n * TOK:(n + 1) * TOK]
                if r == 0 and s == 0:
                    key_at = lax.broadcasted_iota(jnp.int32, (TOK, QCOLS), 0)
                    token = lax.rem(lax.broadcasted_iota(jnp.int32, (TOK, QCOLS), 1), TOK)
                    part = jnp.where(key_at <= token, part, FAR)
                else:
                    seen = position(x, lax.rem(y - r + NY, NY)) <= query_at
                    part = part + jnp.where(seen, 0.0, FAR).astype(F32)
                parts.append(part)
            for n, part in enumerate(parts):
                scores[c * CHUNK + n * TOK:c * CHUNK + (n + 1) * TOK, cols] = part
            top = jnp.maximum(fold_rows(parts[0], jnp.max), fold_rows(parts[1], jnp.max))
            max8[:, cols] = top if c == 0 else jnp.maximum(max8[:, cols], top)

    start(k_go, 2)
    start(k_go, 1)
    loads[0].wait()
    for h in range(HEADS):
        q_t[0, :, h * TOK:(h + 1) * TOK] = q_own[:, h * HD:(h + 1) * HD].T * (SCALE * LOG2E)
    for n in (1, 0, 2):
        q_go[n].start()
    start(v_go, 1)
    loads[1].wait()
    for h in range(HEADS):
        g_t[0, :, h * TOK:(h + 1) * TOK] = g_own[:, h * HD:(h + 1) * HD].T
    for n in (1, 0, 2):
        g_go[n].start()
    for load in loads[2:]:
        load.wait()
    ready_query(0)
    ready_key(OWN)
    ready_cotangent(0)
    ready_value(OWN)

    arrived(k_go, 2)
    start(k_go, 4)
    start(k_go, 3)
    ready_key(0)
    ready_key(1)
    arrived(k_go, 1)
    ready_key(2)
    ready_key(3)
    q_go[0].wait_recv()
    ready_query(1)
    q_go[2].wait_recv()
    ready_query(3)
    arrived(v_go, 1)
    start(v_go, 2)
    q_go[1].wait_recv()
    ready_query(2)
    score_chunk(0)
    score_chunk(1)
    arrived(k_go, 3)
    ready_key(4)
    ready_key(5)
    score_chunk(2)
    arrived(k_go, 4)
    ready_key(7)
    score_chunk(3)
    arrived(v_go, 2)
    start(v_go, 4)
    start(v_go, 3)

    top = jnp.max(max8[...], axis=0, keepdims=True)
    def soft_chunk(c):
        rows = pl.ds(c * CHUNK, CHUNK)
        for s in range(NX):
            cols = pl.ds(s * QCOLS, QCOLS)
            weight = jnp.exp2(scores[rows, cols] - top[:, s * QCOLS:(s + 1) * QCOLS])
            scores[rows, cols] = weight
            high, low = split2(weight)
            p_hi[rows, cols] = high
            p_lo[rows, cols] = low
            part = fold_rows(weight, jnp.sum)
            sum8[:, cols] = part if c == 0 else sum8[:, cols] + part

    for c in range(NY // 2):
        soft_chunk(c)
    stats[0, 0:1, :] = top
    stats[0, 1:2, :] = jnp.sum(sum8[...], axis=0, keepdims=True)
    st_go = [
        remote(stats.at[0], stats.at[n + 1], st_s.at[n], st_r.at[n], peers[n]) for n in range(NX - 1)
    ]
    for copy in st_go:
        copy.start()

    for place in range(4):
        ready_value(place)
    for n in range(NX - 1):
        g_go[n].wait_recv()
        ready_cotangent(n + 1)

    def weigh_chunk(c):
        rows = pl.ds(c * CHUNK, CHUNK)
        for s in range(NX):
            cols = pl.ds(s * QCOLS, QCOLS)
            tile = matmul(vp[rows, :], gs[:, cols])
            gw[rows, cols] = tile
            part = fold_rows(tile * scores[rows, cols], jnp.sum)
            dot8[:, cols] = part if c == 0 else dot8[:, cols] + part

    weigh_chunk(0)
    weigh_chunk(1)

    def aligned(row, n):
        cut = ALLQ - (n + 1) * QCOLS
        return jnp.concatenate([row[:, cut:], row[:, :cut]], axis=1)

    for copy in st_go:
        copy.wait_recv()
    tops = [aligned(stats[n + 1, 0:1, :], n) for n in range(NX - 1)]
    whole_top = jnp.maximum(jnp.maximum(top, tops[0]), jnp.maximum(tops[1], tops[2]))
    own_factor = jnp.exp2(top - whole_top)
    total = own_factor * stats[0, 1:2, :]
    for n in range(NX - 1):
        total = total + jnp.exp2(tops[n] - whole_top) * aligned(stats[n + 1, 1:2, :], n)
    factor = own_factor / total
    scaled[...] = factor

    for s in range(NX):
        cols = pl.ds(s * QCOLS, QCOLS)
        row = scaled[:, cols]
        high, low = split2(g_t[s] * row)
        gf[0:HD, cols] = high
        gf[HD:2 * HD, cols] = low
        high, low = split2(q_t[s] * row)
        qf[0:HD, cols] = high
        qf[HD:2 * HD, cols] = low

    def key_side(c, high, low, right_side, part):
        rows = pl.ds(c * CHUNK, CHUNK)
        both = matmul_nt(high[rows, :], right_side[...]) + matmul_nt(low[rows, :], right_side[...])
        whole = both[:, :HD] + both[:, HD:]
        part[2 * c] = whole[:TOK]
        part[2 * c + 1] = whole[TOK:]

    def back_y(part, whole_in, half_in, send, recv, by_two):
        copies = {}
        for d, (sign, near, far) in enumerate(ways):
            at = [part.at[PLACE[(-sign * n) % NY]] for n in range(5)]
            rows = pl.ds(d * HALF, HALF)
            sems = [(send.at[4 * d + n], recv.at[4 * d + n]) for n in range(4)]
            copies[d, 4] = remote(at[4].at[rows], half_in.at[d], *sems[3], far)
            copies[d, 3] = remote(at[3], whole_in.at[d], *sems[2], near)
            copies[d, 2] = remote(at[2], whole_in.at[2 + d], *sems[1], far if by_two else near)
            copies[d, 1] = remote(at[1], whole_in.at[4 + d], *sems[0], near)
        return copies

    def join_far(copies, part, whole_in, half_in):
        for d, (sign, _, _) in enumerate(ways):
            place = PLACE[(-sign * 2) % NY]
            copies[d, 3].wait_recv()
            part[place] = part[place] + whole_in[d]
            copies[d, 4].wait_recv()
            rows = pl.ds(d * HALF, HALF)
            part[place, rows, :] = part[place, rows, :] + half_in[d]
            copies[d, 2].start()

    def join_near(copies, part, whole_in):
        for d, (sign, _, _) in enumerate(ways):
            place = PLACE[(-sign) % NY]
            copies[d, 2].wait_recv()
            part[place] = part[place] + whole_in[2 + d]
            copies[d, 1].start()

    def back_x(part, into, send, recv):
        return [
            remote(part.at[NX - 1 - n], into.at[n], send.at[n], recv.at[n], peers[n]) for n in range(NX - 1)
        ]

    dv_go = back_y(dv_part, dv_in, dv_half, dvy_s, dvy_r, False)
    dk_go = back_y(dk_part, dk_in, dk_half, dky_s, dky_r, True)
    o_go = back_x(o_part, o_in, ox_s, ox_r)
    dq_go = back_x(dq_part, dq_in, dqx_s, dqx_r)
    everything += [*dv_go.values(), *dk_go.values(), *o_go, *dq_go]

    key_side(2, p_hi, p_lo, gf, dv_part)
    start(dv_go, 3)
    key_side(3, p_hi, p_lo, gf, dv_part)
    start(dv_go, 4)
    key_side(0, p_hi, p_lo, gf, dv_part)

    arrived(v_go, 3)
    ready_value(4)
    ready_value(5)
    weigh_chunk(2)
    arrived(v_go, 4)
    ready_value(7)
    weigh_chunk(3)
    dots[0] = jnp.sum(dot8[...], axis=0, keepdims=True) * scaled[...]
    rd_go = [
        remote(dots.at[0], dots.at[n + 1], rd_s.at[n], rd_r.at[n], peers[n]) for n in range(NX - 1)
    ]
    everything += rd_go
    for copy in rd_go:
        copy.start()
    key_side(1, p_hi, p_lo, gf, dv_part)

    def query_side(s, sides, high, low, part, scale):
        cols = pl.ds(s * QCOLS, QCOLS)
        both = matmul(sides[...], high[:, cols]) + matmul(sides[...], low[:, cols])
        part[s] = (both[:HD] + both[HD:]) * (scaled[:, cols] * scale)

    for n in (1, 0, 2):
        query_side(NX - 1 - n, vt, p_hi, p_lo, o_part, 1.0)
        o_go[n].start()
    query_side(0, vt, p_hi, p_lo, o_part, 1.0)

    for copy in [*gathered, *st_go]:
        copy.wait_send()
    for copy in rd_go:
        copy.wait_recv()
    row_dot = dots[0]
    for n in range(NX - 1):
        row_dot = row_dot + aligned(dots[n + 1], n)

    def grad_chunk(c):
        rows = pl.ds(c * CHUNK, CHUNK)
        for s in range(NX):
            cols = pl.ds(s * QCOLS, QCOLS)
            value = scores[rows, cols] * (gw[rows, cols] - row_dot[:, s * QCOLS:(s + 1) * QCOLS])
            high, low = split2(value)
            t_hi[rows, cols] = high
            t_lo[rows, cols] = low

    grad_chunk(2)
    key_side(2, t_hi, t_lo, qf, dk_part)
    start(dk_go, 3)
    grad_chunk(3)
    key_side(3, t_hi, t_lo, qf, dk_part)
    start(dk_go, 4)
    join_far(dv_go, dv_part, dv_in, dv_half)
    grad_chunk(0)
    key_side(0, t_hi, t_lo, qf, dk_part)
    grad_chunk(1)
    for n in (1, 0, 2):
        query_side(NX - 1 - n, kt, t_hi, t_lo, dq_part, SCALE)
        dq_go[n].start()
    key_side(1, t_hi, t_lo, qf, dk_part)
    start(dk_go, 1)
    join_far(dk_go, dk_part, dk_in, dk_half)
    join_near(dv_go, dv_part, dv_in)
    query_side(0, kt, t_hi, t_lo, dq_part, SCALE)

    def finish_x(copies, part, full_in, out):
        for copy in copies:
            copy.wait_recv()
        whole = (part[0] + full_in[0]) + (full_in[1] + full_in[2])
        for h in range(HEADS):
            out[0, :, h * HD:(h + 1) * HD] = whole[:, h * TOK:(h + 1) * TOK].T

    finish_x(o_go, o_part, o_in, o_out)
    arrived(dv_go, 1)
    dv_out[0] = dv_part[OWN] + (dv_in[4] + dv_in[5])
    finish_x(dq_go, dq_part, dq_in, dq_out)
    arrived(dk_go, 2)
    arrived(dk_go, 1)
    dk_out[0] = (dk_part[OWN] + ((dk_in[2] + dk_in[3]) + (dk_in[4] + dk_in[5]))) * LN2
    for copy in everything:
        copy.wait_send()


def store(*refs):
    sources, targets, sems = refs[:4], refs[4:8], refs[8]
    copies = [pltpu.make_async_copy(a, b, sems.at[n]) for n, (a, b) in enumerate(zip(sources, targets))]
    for copy in copies:
        copy.start()
    for copy in copies:
        copy.wait()


def body(queries, key_rows, value_rows, cotangent, block_order):
    def vmem(*shape, dtype=F32):
        return pltpu.VMEM(shape, dtype)

    dma = lambda n: pltpu.SemaphoreType.DMA((n,))
    in_vmem = pl.BlockSpec(memory_space=pltpu.VMEM)
    in_hbm = pl.BlockSpec(memory_space=pltpu.HBM)
    wide = jax.ShapeDtypeStruct((1, TOK, HEADS * HD), F32)
    narrow = jax.ShapeDtypeStruct((1, TOK, HD), F32)
    shapes = (wide, wide, narrow, narrow)
    results = pl.pallas_call(
        kernel,
        out_shape=shapes,
        in_specs=[in_hbm] * 5,
        out_specs=[in_vmem] * 4,
        scratch_shapes=[
            pltpu.SMEM((NX * NY,), jnp.int32), vmem(TOK, HEADS * HD), vmem(TOK, HEADS * HD),
            vmem(NX, HD, QCOLS), vmem(NX, HD, QCOLS),
            vmem(NY, TOK, HD), vmem(NY, TOK, HD),
            vmem(6 * HD, ALLQ, dtype=BF16), vmem(3 * HD, ALLQ, dtype=BF16),
            vmem(ALLK, 6 * HD, dtype=BF16), vmem(ALLK, 3 * HD, dtype=BF16),
            vmem(2 * HD, ALLK, dtype=BF16), vmem(2 * HD, ALLK, dtype=BF16),
            vmem(2 * HD, ALLQ, dtype=BF16), vmem(2 * HD, ALLQ, dtype=BF16),
            vmem(ALLK, ALLQ), vmem(ALLK, ALLQ),
            vmem(ALLK, ALLQ, dtype=BF16), vmem(ALLK, ALLQ, dtype=BF16),
            vmem(ALLK, ALLQ, dtype=BF16), vmem(ALLK, ALLQ, dtype=BF16),
            vmem(8, ALLQ), vmem(8, ALLQ), vmem(8, ALLQ),
            vmem(NX, 2, ALLQ), vmem(NX, 1, ALLQ), vmem(1, ALLQ),
            vmem(NY, TOK, HD), vmem(NY, TOK, HD),
            vmem(NX, HD, QCOLS), vmem(NX, HD, QCOLS),
            vmem(6, TOK, HD), vmem(2, HALF, HD), vmem(6, TOK, HD), vmem(2, HALF, HD),
            vmem(3, HD, QCOLS), vmem(3, HD, QCOLS),
            dma(5),
            dma(3), dma(3), dma(3), dma(3), dma(8), dma(8), dma(8), dma(8),
            dma(3), dma(3), dma(3), dma(3),
            dma(8), dma(8), dma(8), dma(8), dma(3), dma(3), dma(3), dma(3),
        ],
        compiler_params=pltpu.CompilerParams(
            collective_id=0, has_side_effects=True, vmem_limit_bytes=44 * 1024 * 1024
        ),
    )(*(pltpu.with_memory_space_constraint(a, pltpu.HBM) for a in (block_order, queries, key_rows, value_rows, cotangent)))
    return pl.pallas_call(
        store,
        out_shape=shapes,
        in_specs=[in_vmem] * 4,
        out_specs=[in_hbm] * 4,
        scratch_shapes=[dma(4)],
    )(*(pltpu.with_memory_space_constraint(a, pltpu.VMEM) for a in results))


def solution(mesh):
    spread = P("outer", "inner", None)
    return jax.shard_map(
        body,
        mesh=mesh,
        in_specs=(spread, spread, spread, spread, P()),
        out_specs=(spread, spread, spread, spread),
        check_vma=False,
    )
```

```python
import jax
import jax.numpy as jnp
from jax import lax
from jax.experimental import pallas as pl
from jax.experimental.pallas import tpu as pltpu
from jax.sharding import PartitionSpec as P

HD = 128
HEADS = 2
GROUPS = 4
TOK = 128
NX = 4
NY = 8
QCOLS = HEADS * TOK
ALLQ = NX * QCOLS
ALLK = NY * TOK
HALF = TOK // 2
SCALE = HD ** (-0.5)
LOG2E = 1.4426950408889634
LN2 = 0.6931471805599453
FAR = -1e30
MESH = pl.DeviceIdType.MESH
F32 = jnp.float32
BF16 = jnp.bfloat16

AT = (2, 6, 1, 7, 3, 5, 0, 4)
PLACE = tuple(AT.index(r) for r in range(NY))
OWN = PLACE[0]
CHUNK = 2 * TOK


def split2(value):
    high = value.astype(BF16)
    return high, (value - high.astype(F32)).astype(BF16)


def split3(value):
    high = value.astype(BF16)
    rest = value - high.astype(F32)
    mid = rest.astype(BF16)
    return high, mid, (rest - mid.astype(F32)).astype(BF16)


def matmul(left, right):
    return jnp.dot(left, right, preferred_element_type=F32)


def matmul_nt(left, right):
    return lax.dot_general(left, right, (((1,), (1,)), ((), ())), preferred_element_type=F32)


def fold_rows(value, combine):
    return combine(value.reshape(value.shape[0] // 8, 8, value.shape[1]), axis=0)


def kernel(
    order_hbm, q_hbm, k_hbm, v_hbm, g_hbm, o_out, dq_out, dk_out, dv_out,
    order, q_own, g_own, q_t, g_t, keys, vals, qs, gs, kp, vp, kt, vt, qf, gf,
    scores, gw, p_hi, p_lo, t_hi, t_lo, max8, sum8, dot8, stats, dots, scaled,
    dv_part, dk_part, o_part, dq_part, dv_in, dv_half, dk_in, dk_half, o_in, dq_in,
    local_sem, qx_s, qx_r, gx_s, gx_r, ky_s, ky_r, vy_s, vy_r, st_s, st_r, rd_s, rd_r,
    dvy_s, dvy_r, dky_s, dky_r, ox_s, ox_r, dqx_s, dqx_r,
):
    seqs = lax.axis_size("outer") // GROUPS
    outer = lax.axis_index("outer")
    inner = lax.axis_index("inner")
    seq = lax.rem(outer, seqs)
    x = lax.rem(inner, NX)
    y = (inner // NX) * GROUPS + outer // seqs

    def device(at_x, at_y):
        return (lax.rem(at_y, GROUPS) * seqs + seq, (at_y // GROUPS) * NX + at_x)

    def along_x(step):
        return device(lax.rem(x + step + NX, NX), y)

    def along_y(step):
        return device(x, lax.rem(y + step + NY, NY))

    def position(at_x, at_y):
        return order[lax.rem(at_y, GROUPS) * (NX * NY // GROUPS) + (at_y // GROUPS) * NX + at_x]

    def remote(src, dst, send, recv, where):
        return pltpu.make_async_remote_copy(
            src_ref=src, dst_ref=dst, send_sem=send, recv_sem=recv, device_id=where, device_id_type=MESH
        )

    up, down, up2, down2 = along_y(1), along_y(-1), along_y(2), along_y(-2)
    right, left, across = along_x(1), along_x(-1), along_x(2)
    peers = (right, across, left)

    loads = [
        pltpu.make_async_copy(q_hbm.at[0], q_own, local_sem.at[0]),
        pltpu.make_async_copy(g_hbm.at[0], g_own, local_sem.at[1]),
        pltpu.make_async_copy(k_hbm.at[0], keys.at[OWN], local_sem.at[2]),
        pltpu.make_async_copy(v_hbm.at[0], vals.at[OWN], local_sem.at[3]),
        pltpu.make_async_copy(order_hbm, order, local_sem.at[4]),
    ]
    for load in loads:
        load.start()
    barrier = pltpu.get_barrier_semaphore()
    for peer in (up, down, up2, down2, right, left, across):
        pl.semaphore_signal(barrier, inc=1, device_id=peer, device_id_type=MESH)
    pl.semaphore_wait(barrier, 7)

    ways = ((1, up, up2), (-1, down, down2))

    def gather_y(own, buf, send, recv, by_two):
        copies = {}
        for d, (sign, near, far) in enumerate(ways):
            at = [buf.at[PLACE[(sign * n) % NY]] for n in range(5)]
            rows = pl.ds(d * HALF, HALF)
            copies[d, 1] = remote(own, at[1], send.at[4 * d], recv.at[4 * d], near)
            if by_two:
                copies[d, 2] = remote(own, at[2], send.at[4 * d + 1], recv.at[4 * d + 1], far)
            else:
                copies[d, 2] = remote(at[1], at[2], send.at[4 * d + 1], recv.at[4 * d + 1], near)
            copies[d, 3] = remote(at[2], at[3], send.at[4 * d + 2], recv.at[4 * d + 2], near)
            copies[d, 4] = remote(at[2].at[rows], at[4].at[rows], send.at[4 * d + 3], recv.at[4 * d + 3], far)
        return copies

    def gather_x(buf, send, recv):
        return [
            remote(buf.at[0], buf.at[n + 1], send.at[n], recv.at[n], peers[n]) for n in range(NX - 1)
        ]

    k_go, v_go = gather_y(k_hbm.at[0], keys, ky_s, ky_r, True), gather_y(v_hbm.at[0], vals, vy_s, vy_r, False)
    q_go, g_go = gather_x(q_t, qx_s, qx_r), gather_x(g_t, gx_s, gx_r)
    gathered = [*k_go.values(), *v_go.values(), *q_go, *g_go]
    everything = []

    def start(copies, n):
        for d in range(2):
            copies[d, n].start()

    def arrived(copies, n):
        for d in range(2):
            copies[d, n].wait_recv()

    def ready_query(s):
        cols = pl.ds(s * QCOLS, QCOLS)
        q0, q1, q2 = split3(q_t[s])
        for n, piece in enumerate((q0, q1, q0, q1, q0, q2)):
            qs[n * HD:(n + 1) * HD, cols] = piece

    def ready_cotangent(s):
        cols = pl.ds(s * QCOLS, QCOLS)
        g0, g1 = split2(g_t[s])
        for n, piece in enumerate((g0, g1, g0)):
            gs[n * HD:(n + 1) * HD, cols] = piece

    def ready_key(place):
        rows = pl.ds(place * TOK, TOK)
        k0, k1, k2 = split3(keys[place])
        for n, piece in enumerate((k0, k0, k1, k1, k2, k0)):
            kp[rows, n * HD:(n + 1) * HD] = piece
        high, low = split2(keys[place].T)
        kt[0:HD, rows] = high
        kt[HD:2 * HD, rows] = low

    def ready_value(place):
        rows = pl.ds(place * TOK, TOK)
        v0, v1 = split2(vals[place])
        for n, piece in enumerate((v0, v0, v1)):
            vp[rows, n * HD:(n + 1) * HD] = piece
        high, low = split2(vals[place].T)
        vt[0:HD, rows] = high
        vt[HD:2 * HD, rows] = low

    def score_chunk(c):
        rows = pl.ds(c * CHUNK, CHUNK)
        for s in range(NX):
            cols = pl.ds(s * QCOLS, QCOLS)
            query_at = position(lax.rem(x - s + NX, NX), y)
            tile = matmul(kp[rows, :], qs[:, cols])
            parts = []
            for n in range(2):
                r = AT[2 * c + n]
                part = tile[n * TOK:(n + 1) * TOK]
                if r == 0 and s == 0:
                    key_at = lax.broadcasted_iota(jnp.int32, (TOK, QCOLS), 0)
                    token = lax.rem(lax.broadcasted_iota(jnp.int32, (TOK, QCOLS), 1), TOK)
                    part = jnp.where(key_at <= token, part, FAR)
                else:
                    seen = position(x, lax.rem(y - r + NY, NY)) <= query_at
                    part = part + jnp.where(seen, 0.0, FAR).astype(F32)
                parts.append(part)
            for n, part in enumerate(parts):
                scores[c * CHUNK + n * TOK:c * CHUNK + (n + 1) * TOK, cols] = part
            top = jnp.maximum(fold_rows(parts[0], jnp.max), fold_rows(parts[1], jnp.max))
            max8[:, cols] = top if c == 0 else jnp.maximum(max8[:, cols], top)

    start(k_go, 2)
    start(k_go, 1)
    loads[0].wait()
    for h in range(HEADS):
        q_t[0, :, h * TOK:(h + 1) * TOK] = q_own[:, h * HD:(h + 1) * HD].T * (SCALE * LOG2E)
    for n in (1, 0, 2):
        q_go[n].start()
    start(v_go, 1)
    loads[1].wait()
    for h in range(HEADS):
        g_t[0, :, h * TOK:(h + 1) * TOK] = g_own[:, h * HD:(h + 1) * HD].T
    for load in loads[2:]:
        load.wait()
    ready_query(0)
    ready_key(OWN)
    ready_cotangent(0)
    ready_value(OWN)

    arrived(k_go, 2)
    start(k_go, 4)
    start(k_go, 3)
    ready_key(0)
    ready_key(1)
    arrived(k_go, 1)
    ready_key(2)
    ready_key(3)
    arrived(v_go, 1)
    start(v_go, 2)
    q_go[0].wait_recv()
    ready_query(1)
    q_go[2].wait_recv()
    ready_query(3)
    q_go[1].wait_recv()
    for n in (1, 0, 2):
        g_go[n].start()
    ready_query(2)
    score_chunk(0)
    score_chunk(1)
    arrived(k_go, 3)
    ready_key(4)
    ready_key(5)
    score_chunk(2)
    arrived(k_go, 4)
    arrived(v_go, 2)
    start(v_go, 4)
    start(v_go, 3)
    ready_key(7)
    score_chunk(3)
    top = jnp.max(max8[...], axis=0, keepdims=True)
    def soft_chunk(c):
        rows = pl.ds(c * CHUNK, CHUNK)
        for s in range(NX):
            cols = pl.ds(s * QCOLS, QCOLS)
            weight = jnp.exp2(scores[rows, cols] - top[:, s * QCOLS:(s + 1) * QCOLS])
            scores[rows, cols] = weight
            high, low = split2(weight)
            p_hi[rows, cols] = high
            p_lo[rows, cols] = low
            part = fold_rows(weight, jnp.sum)
            sum8[:, cols] = part if c == 0 else sum8[:, cols] + part

    for c in range(NY // 2):
        soft_chunk(c)
    stats[0, 0:1, :] = top
    stats[0, 1:2, :] = jnp.sum(sum8[...], axis=0, keepdims=True)
    st_go = [
        remote(stats.at[0], stats.at[n + 1], st_s.at[n], st_r.at[n], peers[n]) for n in range(NX - 1)
    ]
    for copy in st_go:
        copy.start()

    for place in range(4):
        ready_value(place)
    for n in range(NX - 1):
        g_go[n].wait_recv()
        ready_cotangent(n + 1)

    def weigh_chunk(c):
        rows = pl.ds(c * CHUNK, CHUNK)
        for s in range(NX):
            cols = pl.ds(s * QCOLS, QCOLS)
            tile = matmul(vp[rows, :], gs[:, cols])
            gw[rows, cols] = tile
            part = fold_rows(tile * scores[rows, cols], jnp.sum)
            dot8[:, cols] = part if c == 0 else dot8[:, cols] + part

    weigh_chunk(0)
    weigh_chunk(1)

    def aligned(row, n):
        cut = ALLQ - (n + 1) * QCOLS
        return jnp.concatenate([row[:, cut:], row[:, :cut]], axis=1)

    for copy in st_go:
        copy.wait_recv()
    tops = [aligned(stats[n + 1, 0:1, :], n) for n in range(NX - 1)]
    whole_top = jnp.maximum(jnp.maximum(top, tops[0]), jnp.maximum(tops[1], tops[2]))
    own_factor = jnp.exp2(top - whole_top)
    total = own_factor * stats[0, 1:2, :]
    for n in range(NX - 1):
        total = total + jnp.exp2(tops[n] - whole_top) * aligned(stats[n + 1, 1:2, :], n)
    factor = own_factor / total
    scaled[...] = factor

    for s in range(NX):
        cols = pl.ds(s * QCOLS, QCOLS)
        row = scaled[:, cols]
        high, low = split2(g_t[s] * row)
        gf[0:HD, cols] = high
        gf[HD:2 * HD, cols] = low

    def key_side(c, high, low, right_side, part):
        rows = pl.ds(c * CHUNK, CHUNK)
        both = matmul_nt(high[rows, :], right_side[...]) + matmul_nt(low[rows, :], right_side[...])
        whole = both[:, :HD] + both[:, HD:]
        part[2 * c] = whole[:TOK]
        part[2 * c + 1] = whole[TOK:]

    def back_y(part, whole_in, half_in, send, recv, by_two):
        copies = {}
        for d, (sign, near, far) in enumerate(ways):
            at = [part.at[PLACE[(-sign * n) % NY]] for n in range(5)]
            rows = pl.ds(d * HALF, HALF)
            sems = [(send.at[4 * d + n], recv.at[4 * d + n]) for n in range(4)]
            copies[d, 4] = remote(at[4].at[rows], half_in.at[d], *sems[3], far)
            copies[d, 3] = remote(at[3], whole_in.at[d], *sems[2], near)
            copies[d, 2] = remote(at[2], whole_in.at[2 + d], *sems[1], far if by_two else near)
            copies[d, 1] = remote(at[1], whole_in.at[4 + d], *sems[0], near)
        return copies

    def join_far(copies, part, whole_in, half_in):
        for d, (sign, _, _) in enumerate(ways):
            place = PLACE[(-sign * 2) % NY]
            copies[d, 3].wait_recv()
            part[place] = part[place] + whole_in[d]
            copies[d, 4].wait_recv()
            rows = pl.ds(d * HALF, HALF)
            part[place, rows, :] = part[place, rows, :] + half_in[d]
            copies[d, 2].start()

    def join_near(copies, part, whole_in):
        for d, (sign, _, _) in enumerate(ways):
            place = PLACE[(-sign) % NY]
            copies[d, 2].wait_recv()
            part[place] = part[place] + whole_in[2 + d]
            copies[d, 1].start()

    def back_x(part, into, send, recv):
        return [
            remote(part.at[NX - 1 - n], into.at[n], send.at[n], recv.at[n], peers[n]) for n in range(NX - 1)
        ]

    dv_go = back_y(dv_part, dv_in, dv_half, dvy_s, dvy_r, False)
    dk_go = back_y(dk_part, dk_in, dk_half, dky_s, dky_r, True)
    o_go = back_x(o_part, o_in, ox_s, ox_r)
    dq_go = back_x(dq_part, dq_in, dqx_s, dqx_r)
    everything += [*dv_go.values(), *dk_go.values(), *o_go, *dq_go]

    arrived(v_go, 3)
    ready_value(4)
    ready_value(5)
    weigh_chunk(2)
    arrived(v_go, 4)
    ready_value(7)
    weigh_chunk(3)
    dots[0] = jnp.sum(dot8[...], axis=0, keepdims=True) * scaled[...]
    rd_go = [
        remote(dots.at[0], dots.at[n + 1], rd_s.at[n], rd_r.at[n], peers[n]) for n in range(NX - 1)
    ]
    everything += rd_go
    for copy in rd_go:
        copy.start()
    key_side(2, p_hi, p_lo, gf, dv_part)
    start(dv_go, 3)
    key_side(3, p_hi, p_lo, gf, dv_part)
    start(dv_go, 4)
    key_side(0, p_hi, p_lo, gf, dv_part)
    for s in range(NX):
        cols = pl.ds(s * QCOLS, QCOLS)
        high, low = split2(q_t[s] * scaled[:, cols])
        qf[0:HD, cols] = high
        qf[HD:2 * HD, cols] = low

    def query_side(s, sides, high, low, part, scale):
        cols = pl.ds(s * QCOLS, QCOLS)
        both = matmul(sides[...], high[:, cols]) + matmul(sides[...], low[:, cols])
        part[s] = (both[:HD] + both[HD:]) * (scaled[:, cols] * scale)

    for n in (1, 0, 2):
        query_side(NX - 1 - n, vt, p_hi, p_lo, o_part, 1.0)
        o_go[n].start()

    for copy in rd_go:
        copy.wait_recv()
    row_dot = dots[0]
    for n in range(NX - 1):
        row_dot = row_dot + aligned(dots[n + 1], n)

    def grad_chunk(c):
        rows = pl.ds(c * CHUNK, CHUNK)
        for s in range(NX):
            cols = pl.ds(s * QCOLS, QCOLS)
            value = scores[rows, cols] * (gw[rows, cols] - row_dot[:, s * QCOLS:(s + 1) * QCOLS])
            high, low = split2(value)
            t_hi[rows, cols] = high
            t_lo[rows, cols] = low

    grad_chunk(2)
    key_side(2, t_hi, t_lo, qf, dk_part)
    start(dk_go, 3)
    grad_chunk(3)
    key_side(3, t_hi, t_lo, qf, dk_part)
    start(dk_go, 4)
    join_far(dv_go, dv_part, dv_in, dv_half)
    key_side(1, p_hi, p_lo, gf, dv_part)
    grad_chunk(0)
    key_side(0, t_hi, t_lo, qf, dk_part)
    grad_chunk(1)
    for n in (1, 0, 2):
        query_side(NX - 1 - n, kt, t_hi, t_lo, dq_part, SCALE)
        dq_go[n].start()
    key_side(1, t_hi, t_lo, qf, dk_part)
    start(dk_go, 1)
    for copy in [*gathered, *st_go]:
        copy.wait_send()
    join_far(dk_go, dk_part, dk_in, dk_half)
    join_near(dv_go, dv_part, dv_in)
    query_side(0, vt, p_hi, p_lo, o_part, 1.0)
    query_side(0, kt, t_hi, t_lo, dq_part, SCALE)

    def finish_x(copies, part, full_in, out):
        for copy in copies:
            copy.wait_recv()
        whole = (part[0] + full_in[0]) + (full_in[1] + full_in[2])
        for h in range(HEADS):
            out[0, :, h * HD:(h + 1) * HD] = whole[:, h * TOK:(h + 1) * TOK].T

    finish_x(o_go, o_part, o_in, o_out)
    arrived(dv_go, 1)
    dv_out[0] = dv_part[OWN] + (dv_in[4] + dv_in[5])
    finish_x(dq_go, dq_part, dq_in, dq_out)
    arrived(dk_go, 2)
    arrived(dk_go, 1)
    dk_out[0] = (dk_part[OWN] + ((dk_in[2] + dk_in[3]) + (dk_in[4] + dk_in[5]))) * LN2
    for copy in everything:
        copy.wait_send()


def store(*refs):
    sources, targets, sems = refs[:4], refs[4:8], refs[8]
    copies = [pltpu.make_async_copy(a, b, sems.at[n]) for n, (a, b) in enumerate(zip(sources, targets))]
    for copy in copies:
        copy.start()
    for copy in copies:
        copy.wait()


def body(queries, key_rows, value_rows, cotangent, block_order):
    def vmem(*shape, dtype=F32):
        return pltpu.VMEM(shape, dtype)

    dma = lambda n: pltpu.SemaphoreType.DMA((n,))
    in_vmem = pl.BlockSpec(memory_space=pltpu.VMEM)
    in_hbm = pl.BlockSpec(memory_space=pltpu.HBM)
    wide = jax.ShapeDtypeStruct((1, TOK, HEADS * HD), F32)
    narrow = jax.ShapeDtypeStruct((1, TOK, HD), F32)
    shapes = (wide, wide, narrow, narrow)
    results = pl.pallas_call(
        kernel,
        out_shape=shapes,
        in_specs=[in_hbm] * 5,
        out_specs=[in_vmem] * 4,
        scratch_shapes=[
            pltpu.SMEM((NX * NY,), jnp.int32), vmem(TOK, HEADS * HD), vmem(TOK, HEADS * HD),
            vmem(NX, HD, QCOLS), vmem(NX, HD, QCOLS),
            vmem(NY, TOK, HD), vmem(NY, TOK, HD),
            vmem(6 * HD, ALLQ, dtype=BF16), vmem(3 * HD, ALLQ, dtype=BF16),
            vmem(ALLK, 6 * HD, dtype=BF16), vmem(ALLK, 3 * HD, dtype=BF16),
            vmem(2 * HD, ALLK, dtype=BF16), vmem(2 * HD, ALLK, dtype=BF16),
            vmem(2 * HD, ALLQ, dtype=BF16), vmem(2 * HD, ALLQ, dtype=BF16),
            vmem(ALLK, ALLQ), vmem(ALLK, ALLQ),
            vmem(ALLK, ALLQ, dtype=BF16), vmem(ALLK, ALLQ, dtype=BF16),
            vmem(ALLK, ALLQ, dtype=BF16), vmem(ALLK, ALLQ, dtype=BF16),
            vmem(8, ALLQ), vmem(8, ALLQ), vmem(8, ALLQ),
            vmem(NX, 2, ALLQ), vmem(NX, 1, ALLQ), vmem(1, ALLQ),
            vmem(NY, TOK, HD), vmem(NY, TOK, HD),
            vmem(NX, HD, QCOLS), vmem(NX, HD, QCOLS),
            vmem(6, TOK, HD), vmem(2, HALF, HD), vmem(6, TOK, HD), vmem(2, HALF, HD),
            vmem(3, HD, QCOLS), vmem(3, HD, QCOLS),
            dma(5),
            dma(3), dma(3), dma(3), dma(3), dma(8), dma(8), dma(8), dma(8),
            dma(3), dma(3), dma(3), dma(3),
            dma(8), dma(8), dma(8), dma(8), dma(3), dma(3), dma(3), dma(3),
        ],
        compiler_params=pltpu.CompilerParams(
            collective_id=0, has_side_effects=True, vmem_limit_bytes=44 * 1024 * 1024
        ),
    )(*(pltpu.with_memory_space_constraint(a, pltpu.HBM) for a in (block_order, queries, key_rows, value_rows, cotangent)))
    return pl.pallas_call(
        store,
        out_shape=shapes,
        in_specs=[in_vmem] * 4,
        out_specs=[in_hbm] * 4,
        scratch_shapes=[dma(4)],
    )(*(pltpu.with_memory_space_constraint(a, pltpu.VMEM) for a in results))


def solution(mesh):
    spread = P("outer", "inner", None)
    return jax.shard_map(
        body,
        mesh=mesh,
        in_specs=(spread, spread, spread, spread, P()),
        out_specs=(spread, spread, spread, spread),
        check_vma=False,
    )
```

```python
import jax
import jax.numpy as jnp
from jax import lax
from jax.experimental import pallas as pl
from jax.experimental.pallas import tpu as pltpu
from jax.sharding import PartitionSpec as P

HD = 128
HEADS = 2
GROUPS = 4
TOK = 128
NX = 4
NY = 8
QCOLS = HEADS * TOK
ALLQ = NX * QCOLS
ALLK = NY * TOK
HALF = TOK // 2
SCALE = HD ** (-0.5)
LOG2E = 1.4426950408889634
LN2 = 0.6931471805599453
FAR = -1e30
MESH = pl.DeviceIdType.MESH
F32 = jnp.float32
BF16 = jnp.bfloat16

AT = (2, 6, 1, 7, 3, 5, 0, 4)
PLACE = tuple(AT.index(r) for r in range(NY))
OWN = PLACE[0]
CHUNK = 2 * TOK


def split2(value):
    high = value.astype(BF16)
    return high, (value - high.astype(F32)).astype(BF16)


def split3(value):
    high = value.astype(BF16)
    rest = value - high.astype(F32)
    mid = rest.astype(BF16)
    return high, mid, (rest - mid.astype(F32)).astype(BF16)


def matmul(left, right):
    return jnp.dot(left, right, preferred_element_type=F32)


def matmul_nt(left, right):
    return lax.dot_general(left, right, (((1,), (1,)), ((), ())), preferred_element_type=F32)


def fold_rows(value, combine):
    return combine(value.reshape(value.shape[0] // 8, 8, value.shape[1]), axis=0)


def kernel(
    order_hbm, q_hbm, k_hbm, v_hbm, g_hbm, o_out, dq_out, dk_out, dv_out,
    order, q_own, g_own, q_t, g_t, keys, vals, qs, gs, kp, vp, kt, vt, qf, gf,
    scores, gw, p_hi, p_lo, t_hi, t_lo, max8, sum8, dot8, stats, dots, scaled,
    dv_part, dk_part, o_part, dq_part, dv_in, dv_half, dk_in, dk_half, o_in, dq_in,
    local_sem, qx_s, qx_r, gx_s, gx_r, ky_s, ky_r, vy_s, vy_r, st_s, st_r, rd_s, rd_r,
    dvy_s, dvy_r, dky_s, dky_r, ox_s, ox_r, dqx_s, dqx_r,
):
    seqs = lax.axis_size("outer") // GROUPS
    outer = lax.axis_index("outer")
    inner = lax.axis_index("inner")
    seq = lax.rem(outer, seqs)
    x = lax.rem(inner, NX)
    y = (inner // NX) * GROUPS + outer // seqs

    def device(at_x, at_y):
        return (lax.rem(at_y, GROUPS) * seqs + seq, (at_y // GROUPS) * NX + at_x)

    def along_x(step):
        return device(lax.rem(x + step + NX, NX), y)

    def along_y(step):
        return device(x, lax.rem(y + step + NY, NY))

    def position(at_x, at_y):
        return order[lax.rem(at_y, GROUPS) * (NX * NY // GROUPS) + (at_y // GROUPS) * NX + at_x]

    def remote(src, dst, send, recv, where):
        return pltpu.make_async_remote_copy(
            src_ref=src, dst_ref=dst, send_sem=send, recv_sem=recv, device_id=where, device_id_type=MESH
        )

    up, down, up2, down2 = along_y(1), along_y(-1), along_y(2), along_y(-2)
    right, left, across = along_x(1), along_x(-1), along_x(2)
    peers = (right, across, left)

    loads = [
        pltpu.make_async_copy(q_hbm.at[0], q_own, local_sem.at[0]),
        pltpu.make_async_copy(g_hbm.at[0], g_own, local_sem.at[1]),
        pltpu.make_async_copy(k_hbm.at[0], keys.at[OWN], local_sem.at[2]),
        pltpu.make_async_copy(v_hbm.at[0], vals.at[OWN], local_sem.at[3]),
        pltpu.make_async_copy(order_hbm, order, local_sem.at[4]),
    ]
    for load in loads:
        load.start()
    barrier = pltpu.get_barrier_semaphore()
    for peer in (up, down, up2, down2, right, left, across):
        pl.semaphore_signal(barrier, inc=1, device_id=peer, device_id_type=MESH)
    pl.semaphore_wait(barrier, 7)

    ways = ((1, up, up2), (-1, down, down2))

    def gather_y(own, buf, send, recv, by_two):
        copies = {}
        for d, (sign, near, far) in enumerate(ways):
            at = [buf.at[PLACE[(sign * n) % NY]] for n in range(5)]
            rows = pl.ds(d * HALF, HALF)
            copies[d, 1] = remote(own, at[1], send.at[4 * d], recv.at[4 * d], near)
            if by_two:
                copies[d, 2] = remote(own, at[2], send.at[4 * d + 1], recv.at[4 * d + 1], far)
            else:
                copies[d, 2] = remote(at[1], at[2], send.at[4 * d + 1], recv.at[4 * d + 1], near)
            copies[d, 3] = remote(at[2], at[3], send.at[4 * d + 2], recv.at[4 * d + 2], near)
            copies[d, 4] = remote(at[2].at[rows], at[4].at[rows], send.at[4 * d + 3], recv.at[4 * d + 3], far)
        return copies

    def gather_x(buf, send, recv):
        return [
            remote(buf.at[0], buf.at[n + 1], send.at[n], recv.at[n], peers[n]) for n in range(NX - 1)
        ]

    k_go, v_go = gather_y(k_hbm.at[0], keys, ky_s, ky_r, True), gather_y(v_hbm.at[0], vals, vy_s, vy_r, False)
    q_go, g_go = gather_x(q_t, qx_s, qx_r), gather_x(g_t, gx_s, gx_r)
    gathered = [*k_go.values(), *v_go.values(), *q_go, *g_go]

    def start(copies, n):
        for d in range(2):
            copies[d, n].start()

    def arrived(copies, n):
        for d in range(2):
            copies[d, n].wait_recv()

    def ready_query(s):
        cols = pl.ds(s * QCOLS, QCOLS)
        q0, q1, q2 = split3(q_t[s])
        for n, piece in enumerate((q0, q1, q0, q1, q0, q2)):
            qs[n * HD:(n + 1) * HD, cols] = piece

    def ready_cotangent(s):
        cols = pl.ds(s * QCOLS, QCOLS)
        g0, g1 = split2(g_t[s])
        for n, piece in enumerate((g0, g1, g0)):
            gs[n * HD:(n + 1) * HD, cols] = piece

    def ready_key(place):
        rows = pl.ds(place * TOK, TOK)
        k0, k1, k2 = split3(keys[place])
        for n, piece in enumerate((k0, k0, k1, k1, k2, k0)):
            kp[rows, n * HD:(n + 1) * HD] = piece
        high, low = split2(keys[place].T)
        kt[0:HD, rows] = high
        kt[HD:2 * HD, rows] = low

    def ready_value(place):
        rows = pl.ds(place * TOK, TOK)
        v0, v1 = split2(vals[place])
        for n, piece in enumerate((v0, v0, v1)):
            vp[rows, n * HD:(n + 1) * HD] = piece
        high, low = split2(vals[place].T)
        vt[0:HD, rows] = high
        vt[HD:2 * HD, rows] = low

    def score_chunk(c):
        rows = pl.ds(c * CHUNK, CHUNK)
        for s in range(NX):
            cols = pl.ds(s * QCOLS, QCOLS)
            query_at = position(lax.rem(x - s + NX, NX), y)
            tile = matmul(kp[rows, :], qs[:, cols])
            parts = []
            for n in range(2):
                r = AT[2 * c + n]
                part = tile[n * TOK:(n + 1) * TOK]
                if r == 0 and s == 0:
                    key_at = lax.broadcasted_iota(jnp.int32, (TOK, QCOLS), 0)
                    token = lax.rem(lax.broadcasted_iota(jnp.int32, (TOK, QCOLS), 1), TOK)
                    part = jnp.where(key_at <= token, part, FAR)
                else:
                    seen = position(x, lax.rem(y - r + NY, NY)) <= query_at
                    part = part + jnp.where(seen, 0.0, FAR).astype(F32)
                parts.append(part)
            for n, part in enumerate(parts):
                scores[c * CHUNK + n * TOK:c * CHUNK + (n + 1) * TOK, cols] = part
            top = jnp.maximum(fold_rows(parts[0], jnp.max), fold_rows(parts[1], jnp.max))
            max8[:, cols] = top if c == 0 else jnp.maximum(max8[:, cols], top)

    start(k_go, 2)
    start(k_go, 1)
    loads[0].wait()
    for h in range(HEADS):
        q_t[0, :, h * TOK:(h + 1) * TOK] = q_own[:, h * HD:(h + 1) * HD].T * (SCALE * LOG2E)
    for n in (1, 0, 2):
        q_go[n].start()
    start(v_go, 1)
    loads[1].wait()
    for h in range(HEADS):
        g_t[0, :, h * TOK:(h + 1) * TOK] = g_own[:, h * HD:(h + 1) * HD].T
    for load in loads[2:]:
        load.wait()
    ready_query(0)
    ready_key(OWN)
    ready_cotangent(0)
    ready_value(OWN)

    arrived(k_go, 2)
    start(k_go, 4)
    start(k_go, 3)
    ready_key(0)
    ready_key(1)
    arrived(k_go, 1)
    ready_key(2)
    ready_key(3)
    arrived(v_go, 1)
    start(v_go, 2)
    q_go[0].wait_recv()
    ready_query(1)
    q_go[2].wait_recv()
    ready_query(3)
    q_go[1].wait_recv()
    for n in (1, 0, 2):
        g_go[n].start()
    ready_query(2)
    score_chunk(0)
    score_chunk(1)
    arrived(k_go, 3)
    ready_key(4)
    ready_key(5)
    score_chunk(2)
    arrived(k_go, 4)
    arrived(v_go, 2)
    start(v_go, 4)
    start(v_go, 3)
    ready_key(7)
    score_chunk(3)
    top = jnp.max(max8[...], axis=0, keepdims=True)
    def soft_chunk(c):
        rows = pl.ds(c * CHUNK, CHUNK)
        for s in range(NX):
            cols = pl.ds(s * QCOLS, QCOLS)
            weight = jnp.exp2(scores[rows, cols] - top[:, s * QCOLS:(s + 1) * QCOLS])
            scores[rows, cols] = weight
            high, low = split2(weight)
            p_hi[rows, cols] = high
            p_lo[rows, cols] = low
            part = fold_rows(weight, jnp.sum)
            sum8[:, cols] = part if c == 0 else sum8[:, cols] + part

    for c in range(NY // 2):
        soft_chunk(c)
    stats[0, 0:1, :] = top
    stats[0, 1:2, :] = jnp.sum(sum8[...], axis=0, keepdims=True)
    st_go = [
        remote(stats.at[0], stats.at[n + 1], st_s.at[n], st_r.at[n], peers[n]) for n in range(NX - 1)
    ]
    for copy in st_go:
        copy.start()

    for place in range(4):
        ready_value(place)
    for n in range(NX - 1):
        g_go[n].wait_recv()
        ready_cotangent(n + 1)

    def weigh_chunk(c):
        rows = pl.ds(c * CHUNK, CHUNK)
        for s in range(NX):
            cols = pl.ds(s * QCOLS, QCOLS)
            tile = matmul(vp[rows, :], gs[:, cols])
            gw[rows, cols] = tile
            part = fold_rows(tile * scores[rows, cols], jnp.sum)
            dot8[:, cols] = part if c == 0 else dot8[:, cols] + part

    weigh_chunk(0)
    weigh_chunk(1)

    def aligned(row, n):
        cut = ALLQ - (n + 1) * QCOLS
        return jnp.concatenate([row[:, cut:], row[:, :cut]], axis=1)

    for copy in st_go:
        copy.wait_recv()
    tops = [aligned(stats[n + 1, 0:1, :], n) for n in range(NX - 1)]
    whole_top = jnp.maximum(jnp.maximum(top, tops[0]), jnp.maximum(tops[1], tops[2]))
    own_factor = jnp.exp2(top - whole_top)
    total = own_factor * stats[0, 1:2, :]
    for n in range(NX - 1):
        total = total + jnp.exp2(tops[n] - whole_top) * aligned(stats[n + 1, 1:2, :], n)
    factor = own_factor / total
    scaled[...] = factor

    for s in range(NX):
        cols = pl.ds(s * QCOLS, QCOLS)
        row = scaled[:, cols]
        high, low = split2(g_t[s] * row)
        gf[0:HD, cols] = high
        gf[HD:2 * HD, cols] = low

    def key_side(c, high, low, right_side, part):
        rows = pl.ds(c * CHUNK, CHUNK)
        both = matmul_nt(high[rows, :], right_side[...]) + matmul_nt(low[rows, :], right_side[...])
        whole = both[:, :HD] + both[:, HD:]
        part[2 * c] = whole[:TOK]
        part[2 * c + 1] = whole[TOK:]

    def back_y(part, whole_in, half_in, send, recv, by_two):
        copies = {}
        for d, (sign, near, far) in enumerate(ways):
            at = [part.at[PLACE[(-sign * n) % NY]] for n in range(5)]
            rows = pl.ds(d * HALF, HALF)
            sems = [(send.at[4 * d + n], recv.at[4 * d + n]) for n in range(4)]
            copies[d, 4] = remote(at[4].at[rows], half_in.at[d], *sems[3], far)
            copies[d, 3] = remote(at[3], whole_in.at[d], *sems[2], near)
            copies[d, 2] = remote(at[2], whole_in.at[2 + d], *sems[1], far if by_two else near)
            copies[d, 1] = remote(at[1], whole_in.at[4 + d], *sems[0], near)
        return copies

    def join_far(copies, part, whole_in, half_in):
        for d, (sign, _, _) in enumerate(ways):
            place = PLACE[(-sign * 2) % NY]
            copies[d, 3].wait_recv()
            part[place] = part[place] + whole_in[d]
            copies[d, 4].wait_recv()
            rows = pl.ds(d * HALF, HALF)
            part[place, rows, :] = part[place, rows, :] + half_in[d]
            copies[d, 2].start()

    def join_near(copies, part, whole_in):
        for d, (sign, _, _) in enumerate(ways):
            place = PLACE[(-sign) % NY]
            copies[d, 2].wait_recv()
            part[place] = part[place] + whole_in[2 + d]
            copies[d, 1].start()

    def back_halves(part, whole_in, half_in, send, recv):
        copies = {}
        for d, (sign, near, far) in enumerate(ways):
            at = [part.at[PLACE[(-sign * n) % NY]] for n in range(5)]
            sems = [(send.at[6 * d + n], recv.at[6 * d + n]) for n in range(6)]
            copies[d, 1] = remote(at[1], whole_in.at[4 + d], *sems[0], near)
            for n in range(2):
                rows = pl.ds((1 - d if n == 0 else d) * HALF, HALF)
                copies[d, 2, n] = remote(at[2].at[rows], whole_in.at[2 + d, rows], *sems[1 + n], far)
                copies[d, 3, n] = remote(at[3].at[rows], whole_in.at[d, rows], *sems[3 + n], near)
            copies[d, 4] = remote(at[4].at[rows], half_in.at[d], *sems[5], far)
        return copies

    def join_halves(copies, part, whole_in, half_in):
        for n in range(2):
            for d, (sign, _, _) in enumerate(ways):
                place = PLACE[(-sign * 2) % NY]
                rows = pl.ds((1 - d if n == 0 else d) * HALF, HALF)
                copies[d, 3, n].wait_recv()
                whole = part[place, rows, :] + whole_in[d, rows, :]
                if n == 1:
                    copies[d, 4].wait_recv()
                    whole = whole + half_in[d]
                part[place, rows, :] = whole
                copies[d, 2, n].start()

    def back_x(part, into, send, recv):
        return [
            remote(part.at[NX - 1 - n], into.at[n], send.at[n], recv.at[n], peers[n]) for n in range(NX - 1)
        ]

    dv_go = back_y(dv_part, dv_in, dv_half, dvy_s, dvy_r, False)
    dk_go = back_halves(dk_part, dk_in, dk_half, dky_s, dky_r)
    o_go = back_x(o_part, o_in, ox_s, ox_r)
    dq_go = back_x(dq_part, dq_in, dqx_s, dqx_r)

    arrived(v_go, 3)
    ready_value(4)
    ready_value(5)
    weigh_chunk(2)
    arrived(v_go, 4)
    ready_value(7)
    weigh_chunk(3)
    dots[0] = jnp.sum(dot8[...], axis=0, keepdims=True) * scaled[...]
    rd_go = [
        remote(dots.at[0], dots.at[n + 1], rd_s.at[n], rd_r.at[n], peers[n]) for n in range(NX - 1)
    ]
    for copy in rd_go:
        copy.start()
    key_side(3, p_hi, p_lo, gf, dv_part)
    start(dv_go, 4)
    key_side(2, p_hi, p_lo, gf, dv_part)
    start(dv_go, 3)
    key_side(0, p_hi, p_lo, gf, dv_part)
    for s in range(NX):
        cols = pl.ds(s * QCOLS, QCOLS)
        high, low = split2(q_t[s] * scaled[:, cols])
        qf[0:HD, cols] = high
        qf[HD:2 * HD, cols] = low

    def query_side(s, sides, high, low, part, scale):
        cols = pl.ds(s * QCOLS, QCOLS)
        both = matmul(sides[...], high[:, cols]) + matmul(sides[...], low[:, cols])
        part[s] = (both[:HD] + both[HD:]) * (scaled[:, cols] * scale)

    for n in (1, 0, 2):
        query_side(NX - 1 - n, vt, p_hi, p_lo, o_part, 1.0)
        o_go[n].start()

    for copy in rd_go:
        copy.wait_recv()
    row_dot = dots[0]
    for n in range(NX - 1):
        row_dot = row_dot + aligned(dots[n + 1], n)

    def grad_chunk(c):
        rows = pl.ds(c * CHUNK, CHUNK)
        for s in range(NX):
            cols = pl.ds(s * QCOLS, QCOLS)
            value = scores[rows, cols] * (gw[rows, cols] - row_dot[:, s * QCOLS:(s + 1) * QCOLS])
            high, low = split2(value)
            t_hi[rows, cols] = high
            t_lo[rows, cols] = low

    grad_chunk(3)
    key_side(3, t_hi, t_lo, qf, dk_part)
    start(dk_go, 4)
    grad_chunk(2)
    key_side(2, t_hi, t_lo, qf, dk_part)
    for n in range(2):
        for d in range(2):
            dk_go[d, 3, n].start()
    join_far(dv_go, dv_part, dv_in, dv_half)
    grad_chunk(1)
    key_side(1, t_hi, t_lo, qf, dk_part)
    start(dk_go, 1)
    grad_chunk(0)
    key_side(0, t_hi, t_lo, qf, dk_part)
    for n in (1, 0, 2):
        query_side(NX - 1 - n, kt, t_hi, t_lo, dq_part, SCALE)
        dq_go[n].start()
    key_side(1, p_hi, p_lo, gf, dv_part)
    for copy in [*gathered, *st_go]:
        copy.wait_send()
    join_halves(dk_go, dk_part, dk_in, dk_half)
    join_near(dv_go, dv_part, dv_in)
    query_side(0, vt, p_hi, p_lo, o_part, 1.0)
    query_side(0, kt, t_hi, t_lo, dq_part, SCALE)

    def finish_x(copies, part, full_in, out):
        for copy in copies:
            copy.wait_recv()
        whole = (part[0] + full_in[0]) + (full_in[1] + full_in[2])
        for h in range(HEADS):
            out[0, :, h * HD:(h + 1) * HD] = whole[:, h * TOK:(h + 1) * TOK].T

    finish_x(o_go, o_part, o_in, o_out)
    arrived(dv_go, 1)
    dv_out[0] = dv_part[OWN] + (dv_in[4] + dv_in[5])
    for copy in [*rd_go, *dv_go.values(), *o_go]:
        copy.wait_send()
    finish_x(dq_go, dq_part, dq_in, dq_out)
    for n in range(2):
        for d in range(2):
            dk_go[d, 2, n].wait_recv()
    arrived(dk_go, 1)
    dk_out[0] = (dk_part[OWN] + ((dk_in[2] + dk_in[3]) + (dk_in[4] + dk_in[5]))) * LN2
    for copy in [*dq_go, *dk_go.values()]:
        copy.wait_send()


def store(*refs):
    sources, targets, sems = refs[:4], refs[4:8], refs[8]
    copies = [pltpu.make_async_copy(a, b, sems.at[n]) for n, (a, b) in enumerate(zip(sources, targets))]
    for copy in copies:
        copy.start()
    for copy in copies:
        copy.wait()


def body(queries, key_rows, value_rows, cotangent, block_order):
    def vmem(*shape, dtype=F32):
        return pltpu.VMEM(shape, dtype)

    dma = lambda n: pltpu.SemaphoreType.DMA((n,))
    in_vmem = pl.BlockSpec(memory_space=pltpu.VMEM)
    in_hbm = pl.BlockSpec(memory_space=pltpu.HBM)
    wide = jax.ShapeDtypeStruct((1, TOK, HEADS * HD), F32)
    narrow = jax.ShapeDtypeStruct((1, TOK, HD), F32)
    shapes = (wide, wide, narrow, narrow)
    results = pl.pallas_call(
        kernel,
        out_shape=shapes,
        in_specs=[in_hbm] * 5,
        out_specs=[in_vmem] * 4,
        scratch_shapes=[
            pltpu.SMEM((NX * NY,), jnp.int32), vmem(TOK, HEADS * HD), vmem(TOK, HEADS * HD),
            vmem(NX, HD, QCOLS), vmem(NX, HD, QCOLS),
            vmem(NY, TOK, HD), vmem(NY, TOK, HD),
            vmem(6 * HD, ALLQ, dtype=BF16), vmem(3 * HD, ALLQ, dtype=BF16),
            vmem(ALLK, 6 * HD, dtype=BF16), vmem(ALLK, 3 * HD, dtype=BF16),
            vmem(2 * HD, ALLK, dtype=BF16), vmem(2 * HD, ALLK, dtype=BF16),
            vmem(2 * HD, ALLQ, dtype=BF16), vmem(2 * HD, ALLQ, dtype=BF16),
            vmem(ALLK, ALLQ), vmem(ALLK, ALLQ),
            vmem(ALLK, ALLQ, dtype=BF16), vmem(ALLK, ALLQ, dtype=BF16),
            vmem(ALLK, ALLQ, dtype=BF16), vmem(ALLK, ALLQ, dtype=BF16),
            vmem(8, ALLQ), vmem(8, ALLQ), vmem(8, ALLQ),
            vmem(NX, 2, ALLQ), vmem(NX, 1, ALLQ), vmem(1, ALLQ),
            vmem(NY, TOK, HD), vmem(NY, TOK, HD),
            vmem(NX, HD, QCOLS), vmem(NX, HD, QCOLS),
            vmem(6, TOK, HD), vmem(2, HALF, HD), vmem(6, TOK, HD), vmem(2, HALF, HD),
            vmem(3, HD, QCOLS), vmem(3, HD, QCOLS),
            dma(5),
            dma(3), dma(3), dma(3), dma(3), dma(8), dma(8), dma(8), dma(8),
            dma(3), dma(3), dma(3), dma(3),
            dma(8), dma(8), dma(12), dma(12), dma(3), dma(3), dma(3), dma(3),
        ],
        compiler_params=pltpu.CompilerParams(
            collective_id=0, has_side_effects=True, vmem_limit_bytes=44 * 1024 * 1024
        ),
    )(*(pltpu.with_memory_space_constraint(a, pltpu.HBM) for a in (block_order, queries, key_rows, value_rows, cotangent)))
    return pl.pallas_call(
        store,
        out_shape=shapes,
        in_specs=[in_vmem] * 4,
        out_specs=[in_hbm] * 4,
        scratch_shapes=[dma(4)],
    )(*(pltpu.with_memory_space_constraint(a, pltpu.VMEM) for a in results))


def solution(mesh):
    spread = P("outer", "inner", None)
    return jax.shard_map(
        body,
        mesh=mesh,
        in_specs=(spread, spread, spread, spread, P()),
        out_specs=(spread, spread, spread, spread),
        check_vma=False,
    )
```

```python
import jax
import jax.numpy as jnp
from jax import lax
from jax.experimental import pallas as pl
from jax.experimental.pallas import tpu as pltpu
from jax.sharding import PartitionSpec as P

HD = 128
HEADS = 2
GROUPS = 4
TOK = 128
NX = 4
NY = 8
QCOLS = HEADS * TOK
ALLQ = NX * QCOLS
ALLK = NY * TOK
HALF = TOK // 2
SCALE = HD ** (-0.5)
LOG2E = 1.4426950408889634
LN2 = 0.6931471805599453
FAR = -1e30
MESH = pl.DeviceIdType.MESH
F32 = jnp.float32
BF16 = jnp.bfloat16

AT = (2, 6, 1, 7, 3, 5, 0, 4)
PLACE = tuple(AT.index(r) for r in range(NY))
OWN = PLACE[0]
CHUNK = 2 * TOK


def split2(value):
    high = value.astype(BF16)
    return high, (value - high.astype(F32)).astype(BF16)


def split3(value):
    high = value.astype(BF16)
    rest = value - high.astype(F32)
    mid = rest.astype(BF16)
    return high, mid, (rest - mid.astype(F32)).astype(BF16)


def matmul(left, right):
    return jnp.dot(left, right, preferred_element_type=F32)


def matmul_nt(left, right):
    return lax.dot_general(left, right, (((1,), (1,)), ((), ())), preferred_element_type=F32)


def fold_rows(value, combine):
    return combine(value.reshape(value.shape[0] // 8, 8, value.shape[1]), axis=0)


def kernel(
    order_hbm, q_hbm, k_hbm, v_hbm, g_hbm, o_out, dq_out, dk_out, dv_out,
    order, q_own, g_own, q_t, g_t, keys, vals, qs, gs, kp, vp, kt, vt, qf, gf,
    scores, gw, p_hi, p_lo, t_hi, t_lo, max8, sum8, dot8, stats, dots, scaled,
    dv_part, dk_part, o_part, dq_part, dv_in, dv_half, dk_in, dk_half, o_in, dq_in,
    local_sem, qx_s, qx_r, gx_s, gx_r, ky_s, ky_r, vy_s, vy_r, st_s, st_r, rd_s, rd_r,
    dvy_s, dvy_r, dky_s, dky_r, ox_s, ox_r, dqx_s, dqx_r,
):
    seqs = lax.axis_size("outer") // GROUPS
    outer = lax.axis_index("outer")
    inner = lax.axis_index("inner")
    seq = lax.rem(outer, seqs)
    x = lax.rem(inner, NX)
    y = (inner // NX) * GROUPS + outer // seqs

    def device(at_x, at_y):
        return (lax.rem(at_y, GROUPS) * seqs + seq, (at_y // GROUPS) * NX + at_x)

    def along_x(step):
        return device(lax.rem(x + step + NX, NX), y)

    def along_y(step):
        return device(x, lax.rem(y + step + NY, NY))

    def position(at_x, at_y):
        return order[lax.rem(at_y, GROUPS) * (NX * NY // GROUPS) + (at_y // GROUPS) * NX + at_x]

    def remote(src, dst, send, recv, where):
        return pltpu.make_async_remote_copy(
            src_ref=src, dst_ref=dst, send_sem=send, recv_sem=recv, device_id=where, device_id_type=MESH
        )

    up, down, up2, down2 = along_y(1), along_y(-1), along_y(2), along_y(-2)
    right, left, across = along_x(1), along_x(-1), along_x(2)
    peers = (right, across, left)

    loads = [
        pltpu.make_async_copy(q_hbm.at[0], q_own, local_sem.at[0]),
        pltpu.make_async_copy(g_hbm.at[0], g_own, local_sem.at[1]),
        pltpu.make_async_copy(k_hbm.at[0], keys.at[OWN], local_sem.at[2]),
        pltpu.make_async_copy(v_hbm.at[0], vals.at[OWN], local_sem.at[3]),
        pltpu.make_async_copy(order_hbm, order, local_sem.at[4]),
    ]
    for load in loads:
        load.start()
    barrier = pltpu.get_barrier_semaphore()
    for peer in (up, down, up2, down2, right, left, across):
        pl.semaphore_signal(barrier, inc=1, device_id=peer, device_id_type=MESH)
    pl.semaphore_wait(barrier, 7)

    ways = ((1, up, up2), (-1, down, down2))

    def gather_y(own, buf, send, recv, by_two):
        copies = {}
        for d, (sign, near, far) in enumerate(ways):
            at = [buf.at[PLACE[(sign * n) % NY]] for n in range(5)]
            rows = pl.ds(d * HALF, HALF)
            copies[d, 1] = remote(own, at[1], send.at[4 * d], recv.at[4 * d], near)
            if by_two:
                copies[d, 2] = remote(own, at[2], send.at[4 * d + 1], recv.at[4 * d + 1], far)
            else:
                copies[d, 2] = remote(at[1], at[2], send.at[4 * d + 1], recv.at[4 * d + 1], near)
            copies[d, 3] = remote(at[2], at[3], send.at[4 * d + 2], recv.at[4 * d + 2], near)
            copies[d, 4] = remote(at[2].at[rows], at[4].at[rows], send.at[4 * d + 3], recv.at[4 * d + 3], far)
        return copies

    def gather_halves(own, buf, send, recv):
        copies = {}
        for d, (sign, near, far) in enumerate(ways):
            at = [buf.at[PLACE[(sign * n) % NY]] for n in range(5)]
            sems = [(send.at[6 * d + n], recv.at[6 * d + n]) for n in range(6)]
            for n in range(2):
                rows = pl.ds((d if n == 0 else 1 - d) * HALF, HALF)
                copies[d, 1, n] = remote(own.at[rows], at[1].at[rows], *sems[n], near)
                copies[d, 2, n] = remote(at[1].at[rows], at[2].at[rows], *sems[2 + n], near)
            rows = pl.ds(d * HALF, HALF)
            copies[d, 3] = remote(at[2], at[3], *sems[4], near)
            copies[d, 4] = remote(at[2].at[rows], at[4].at[rows], *sems[5], far)
        return copies

    def gather_x(buf, send, recv):
        return [
            remote(buf.at[0], buf.at[n + 1], send.at[n], recv.at[n], peers[n]) for n in range(NX - 1)
        ]

    k_go, v_go = gather_y(k_hbm.at[0], keys, ky_s, ky_r, True), gather_halves(v_hbm.at[0], vals, vy_s, vy_r)
    q_go, g_go = gather_x(q_t, qx_s, qx_r), gather_x(g_t, gx_s, gx_r)
    gathered = [*k_go.values(), *v_go.values(), *q_go, *g_go]

    def start(copies, n):
        for d in range(2):
            copies[d, n].start()

    def arrived(copies, n):
        for d in range(2):
            copies[d, n].wait_recv()

    def ready_query(s):
        cols = pl.ds(s * QCOLS, QCOLS)
        q0, q1, q2 = split3(q_t[s])
        for n, piece in enumerate((q0, q1, q0, q1, q0, q2)):
            qs[n * HD:(n + 1) * HD, cols] = piece

    def ready_cotangent(s):
        cols = pl.ds(s * QCOLS, QCOLS)
        g0, g1 = split2(g_t[s])
        for n, piece in enumerate((g0, g1, g0)):
            gs[n * HD:(n + 1) * HD, cols] = piece

    def ready_key(place):
        rows = pl.ds(place * TOK, TOK)
        k0, k1, k2 = split3(keys[place])
        for n, piece in enumerate((k0, k0, k1, k1, k2, k0)):
            kp[rows, n * HD:(n + 1) * HD] = piece
        high, low = split2(keys[place].T)
        kt[0:HD, rows] = high
        kt[HD:2 * HD, rows] = low

    def ready_value(place):
        rows = pl.ds(place * TOK, TOK)
        v0, v1 = split2(vals[place])
        for n, piece in enumerate((v0, v0, v1)):
            vp[rows, n * HD:(n + 1) * HD] = piece
        high, low = split2(vals[place].T)
        vt[0:HD, rows] = high
        vt[HD:2 * HD, rows] = low

    def score_chunk(c):
        rows = pl.ds(c * CHUNK, CHUNK)
        for s in range(NX):
            cols = pl.ds(s * QCOLS, QCOLS)
            query_at = position(lax.rem(x - s + NX, NX), y)
            tile = matmul(kp[rows, :], qs[:, cols])
            parts = []
            for n in range(2):
                r = AT[2 * c + n]
                part = tile[n * TOK:(n + 1) * TOK]
                if r == 0 and s == 0:
                    key_at = lax.broadcasted_iota(jnp.int32, (TOK, QCOLS), 0)
                    token = lax.rem(lax.broadcasted_iota(jnp.int32, (TOK, QCOLS), 1), TOK)
                    part = jnp.where(key_at <= token, part, FAR)
                else:
                    seen = position(x, lax.rem(y - r + NY, NY)) <= query_at
                    part = part + jnp.where(seen, 0.0, FAR).astype(F32)
                parts.append(part)
            for n, part in enumerate(parts):
                scores[c * CHUNK + n * TOK:c * CHUNK + (n + 1) * TOK, cols] = part
            top = jnp.maximum(fold_rows(parts[0], jnp.max), fold_rows(parts[1], jnp.max))
            max8[:, cols] = top if c == 0 else jnp.maximum(max8[:, cols], top)

    start(k_go, 2)
    start(k_go, 1)
    loads[0].wait()
    for h in range(HEADS):
        q_t[0, :, h * TOK:(h + 1) * TOK] = q_own[:, h * HD:(h + 1) * HD].T * (SCALE * LOG2E)
    for n in (1, 0, 2):
        q_go[n].start()
    for n in range(2):
        for d in range(2):
            v_go[d, 1, n].start()
    loads[1].wait()
    for h in range(HEADS):
        g_t[0, :, h * TOK:(h + 1) * TOK] = g_own[:, h * HD:(h + 1) * HD].T
    for load in loads[2:]:
        load.wait()
    ready_query(0)
    ready_key(OWN)
    ready_cotangent(0)
    ready_value(OWN)

    arrived(k_go, 2)
    start(k_go, 4)
    start(k_go, 3)
    ready_key(0)
    ready_key(1)
    arrived(k_go, 1)
    ready_key(2)
    ready_key(3)
    for n in range(2):
        for d in range(2):
            v_go[d, 1, n].wait_recv()
            v_go[d, 2, n].start()
    q_go[0].wait_recv()
    ready_query(1)
    q_go[2].wait_recv()
    ready_query(3)
    q_go[1].wait_recv()
    for n in (1, 0, 2):
        g_go[n].start()
    ready_query(2)
    score_chunk(0)
    score_chunk(1)
    arrived(k_go, 3)
    ready_key(4)
    ready_key(5)
    score_chunk(2)
    arrived(k_go, 4)
    for n, last in enumerate((4, 3)):
        for d in range(2):
            v_go[d, 2, n].wait_recv()
            v_go[d, last].start()
    ready_key(7)
    score_chunk(3)
    top = jnp.max(max8[...], axis=0, keepdims=True)
    def soft_chunk(c):
        rows = pl.ds(c * CHUNK, CHUNK)
        for s in range(NX):
            cols = pl.ds(s * QCOLS, QCOLS)
            weight = jnp.exp2(scores[rows, cols] - top[:, s * QCOLS:(s + 1) * QCOLS])
            scores[rows, cols] = weight
            high, low = split2(weight)
            p_hi[rows, cols] = high
            p_lo[rows, cols] = low
            part = fold_rows(weight, jnp.sum)
            sum8[:, cols] = part if c == 0 else sum8[:, cols] + part

    for c in range(NY // 2):
        soft_chunk(c)
    stats[0, 0:1, :] = top
    stats[0, 1:2, :] = jnp.sum(sum8[...], axis=0, keepdims=True)
    st_go = [
        remote(stats.at[0], stats.at[n + 1], st_s.at[n], st_r.at[n], peers[n]) for n in range(NX - 1)
    ]
    for copy in st_go:
        copy.start()

    for place in range(4):
        ready_value(place)
    for n in range(NX - 1):
        g_go[n].wait_recv()
        ready_cotangent(n + 1)

    def weigh_chunk(c):
        rows = pl.ds(c * CHUNK, CHUNK)
        for s in range(NX):
            cols = pl.ds(s * QCOLS, QCOLS)
            tile = matmul(vp[rows, :], gs[:, cols])
            gw[rows, cols] = tile
            part = fold_rows(tile * scores[rows, cols], jnp.sum)
            dot8[:, cols] = part if c == 0 else dot8[:, cols] + part

    weigh_chunk(0)
    weigh_chunk(1)

    def aligned(row, n):
        cut = ALLQ - (n + 1) * QCOLS
        return jnp.concatenate([row[:, cut:], row[:, :cut]], axis=1)

    for copy in st_go:
        copy.wait_recv()
    tops = [aligned(stats[n + 1, 0:1, :], n) for n in range(NX - 1)]
    whole_top = jnp.maximum(jnp.maximum(top, tops[0]), jnp.maximum(tops[1], tops[2]))
    own_factor = jnp.exp2(top - whole_top)
    total = own_factor * stats[0, 1:2, :]
    for n in range(NX - 1):
        total = total + jnp.exp2(tops[n] - whole_top) * aligned(stats[n + 1, 1:2, :], n)
    factor = own_factor / total
    scaled[...] = factor

    for s in range(NX):
        cols = pl.ds(s * QCOLS, QCOLS)
        row = scaled[:, cols]
        high, low = split2(g_t[s] * row)
        gf[0:HD, cols] = high
        gf[HD:2 * HD, cols] = low

    def key_side(c, high, low, right_side, part):
        rows = pl.ds(c * CHUNK, CHUNK)
        both = matmul_nt(high[rows, :], right_side[...]) + matmul_nt(low[rows, :], right_side[...])
        whole = both[:, :HD] + both[:, HD:]
        part[2 * c] = whole[:TOK]
        part[2 * c + 1] = whole[TOK:]

    def back_y(part, whole_in, half_in, send, recv, by_two):
        copies = {}
        for d, (sign, near, far) in enumerate(ways):
            at = [part.at[PLACE[(-sign * n) % NY]] for n in range(5)]
            rows = pl.ds(d * HALF, HALF)
            sems = [(send.at[4 * d + n], recv.at[4 * d + n]) for n in range(4)]
            copies[d, 4] = remote(at[4].at[rows], half_in.at[d], *sems[3], far)
            copies[d, 3] = remote(at[3], whole_in.at[d], *sems[2], near)
            copies[d, 2] = remote(at[2], whole_in.at[2 + d], *sems[1], far if by_two else near)
            copies[d, 1] = remote(at[1], whole_in.at[4 + d], *sems[0], near)
        return copies

    def join_far(copies, part, whole_in, half_in):
        for d, (sign, _, _) in enumerate(ways):
            place = PLACE[(-sign * 2) % NY]
            copies[d, 3].wait_recv()
            part[place] = part[place] + whole_in[d]
            copies[d, 4].wait_recv()
            rows = pl.ds(d * HALF, HALF)
            part[place, rows, :] = part[place, rows, :] + half_in[d]
            copies[d, 2].start()

    def join_near(copies, part, whole_in):
        for d, (sign, _, _) in enumerate(ways):
            place = PLACE[(-sign) % NY]
            copies[d, 2].wait_recv()
            part[place] = part[place] + whole_in[2 + d]
            copies[d, 1].start()

    def back_halves(part, whole_in, half_in, send, recv):
        copies = {}
        for d, (sign, near, far) in enumerate(ways):
            at = [part.at[PLACE[(-sign * n) % NY]] for n in range(5)]
            sems = [(send.at[6 * d + n], recv.at[6 * d + n]) for n in range(6)]
            copies[d, 1] = remote(at[1], whole_in.at[4 + d], *sems[0], near)
            for n in range(2):
                rows = pl.ds((1 - d if n == 0 else d) * HALF, HALF)
                copies[d, 2, n] = remote(at[2].at[rows], whole_in.at[2 + d, rows], *sems[1 + n], far)
                copies[d, 3, n] = remote(at[3].at[rows], whole_in.at[d, rows], *sems[3 + n], near)
            copies[d, 4] = remote(at[4].at[rows], half_in.at[d], *sems[5], far)
        return copies

    def join_halves(copies, part, whole_in, half_in):
        for n in range(2):
            for d, (sign, _, _) in enumerate(ways):
                place = PLACE[(-sign * 2) % NY]
                rows = pl.ds((1 - d if n == 0 else d) * HALF, HALF)
                copies[d, 3, n].wait_recv()
                whole = part[place, rows, :] + whole_in[d, rows, :]
                if n == 1:
                    copies[d, 4].wait_recv()
                    whole = whole + half_in[d]
                part[place, rows, :] = whole
                copies[d, 2, n].start()

    def back_x(part, into, send, recv):
        return [
            remote(part.at[NX - 1 - n], into.at[n], send.at[n], recv.at[n], peers[n]) for n in range(NX - 1)
        ]

    dv_go = back_y(dv_part, dv_in, dv_half, dvy_s, dvy_r, False)
    dk_go = back_halves(dk_part, dk_in, dk_half, dky_s, dky_r)
    o_go = back_x(o_part, o_in, ox_s, ox_r)
    dq_go = back_x(dq_part, dq_in, dqx_s, dqx_r)

    arrived(v_go, 3)
    ready_value(4)
    ready_value(5)
    weigh_chunk(2)
    arrived(v_go, 4)
    ready_value(7)
    weigh_chunk(3)
    dots[0] = jnp.sum(dot8[...], axis=0, keepdims=True) * scaled[...]
    rd_go = [
        remote(dots.at[0], dots.at[n + 1], rd_s.at[n], rd_r.at[n], peers[n]) for n in range(NX - 1)
    ]
    for copy in rd_go:
        copy.start()
    key_side(3, p_hi, p_lo, gf, dv_part)
    start(dv_go, 4)
    key_side(2, p_hi, p_lo, gf, dv_part)
    start(dv_go, 3)
    key_side(0, p_hi, p_lo, gf, dv_part)
    for s in range(NX):
        cols = pl.ds(s * QCOLS, QCOLS)
        high, low = split2(q_t[s] * scaled[:, cols])
        qf[0:HD, cols] = high
        qf[HD:2 * HD, cols] = low

    def query_side(s, sides, high, low, part, scale):
        cols = pl.ds(s * QCOLS, QCOLS)
        both = matmul(sides[...], high[:, cols]) + matmul(sides[...], low[:, cols])
        part[s] = (both[:HD] + both[HD:]) * (scaled[:, cols] * scale)

    for n in (1, 0, 2):
        query_side(NX - 1 - n, vt, p_hi, p_lo, o_part, 1.0)
        o_go[n].start()

    for copy in rd_go:
        copy.wait_recv()
    row_dot = dots[0]
    for n in range(NX - 1):
        row_dot = row_dot + aligned(dots[n + 1], n)

    def grad_chunk(c):
        rows = pl.ds(c * CHUNK, CHUNK)
        for s in range(NX):
            cols = pl.ds(s * QCOLS, QCOLS)
            value = scores[rows, cols] * (gw[rows, cols] - row_dot[:, s * QCOLS:(s + 1) * QCOLS])
            high, low = split2(value)
            t_hi[rows, cols] = high
            t_lo[rows, cols] = low

    grad_chunk(3)
    key_side(3, t_hi, t_lo, qf, dk_part)
    start(dk_go, 4)
    grad_chunk(2)
    key_side(2, t_hi, t_lo, qf, dk_part)
    for n in range(2):
        for d in range(2):
            dk_go[d, 3, n].start()
    join_far(dv_go, dv_part, dv_in, dv_half)
    grad_chunk(1)
    key_side(1, t_hi, t_lo, qf, dk_part)
    start(dk_go, 1)
    grad_chunk(0)
    key_side(0, t_hi, t_lo, qf, dk_part)
    for n in (1, 0, 2):
        query_side(NX - 1 - n, kt, t_hi, t_lo, dq_part, SCALE)
        dq_go[n].start()
    key_side(1, p_hi, p_lo, gf, dv_part)
    for copy in [*gathered, *st_go]:
        copy.wait_send()
    join_halves(dk_go, dk_part, dk_in, dk_half)
    join_near(dv_go, dv_part, dv_in)
    query_side(0, vt, p_hi, p_lo, o_part, 1.0)
    query_side(0, kt, t_hi, t_lo, dq_part, SCALE)

    def finish_x(copies, part, full_in, out):
        for copy in copies:
            copy.wait_recv()
        whole = (part[0] + full_in[0]) + (full_in[1] + full_in[2])
        for h in range(HEADS):
            out[0, :, h * HD:(h + 1) * HD] = whole[:, h * TOK:(h + 1) * TOK].T

    finish_x(o_go, o_part, o_in, o_out)
    arrived(dv_go, 1)
    dv_out[0] = dv_part[OWN] + (dv_in[4] + dv_in[5])
    for copy in [*rd_go, *dv_go.values(), *o_go]:
        copy.wait_send()
    finish_x(dq_go, dq_part, dq_in, dq_out)
    for n in range(2):
        for d in range(2):
            dk_go[d, 2, n].wait_recv()
    arrived(dk_go, 1)
    dk_out[0] = (dk_part[OWN] + ((dk_in[2] + dk_in[3]) + (dk_in[4] + dk_in[5]))) * LN2
    for copy in [*dq_go, *dk_go.values()]:
        copy.wait_send()


def store(*refs):
    sources, targets, sems = refs[:4], refs[4:8], refs[8]
    copies = [pltpu.make_async_copy(a, b, sems.at[n]) for n, (a, b) in enumerate(zip(sources, targets))]
    for copy in copies:
        copy.start()
    for copy in copies:
        copy.wait()


def body(queries, key_rows, value_rows, cotangent, block_order):
    def vmem(*shape, dtype=F32):
        return pltpu.VMEM(shape, dtype)

    dma = lambda n: pltpu.SemaphoreType.DMA((n,))
    in_vmem = pl.BlockSpec(memory_space=pltpu.VMEM)
    in_hbm = pl.BlockSpec(memory_space=pltpu.HBM)
    wide = jax.ShapeDtypeStruct((1, TOK, HEADS * HD), F32)
    narrow = jax.ShapeDtypeStruct((1, TOK, HD), F32)
    shapes = (wide, wide, narrow, narrow)
    results = pl.pallas_call(
        kernel,
        out_shape=shapes,
        in_specs=[in_hbm] * 5,
        out_specs=[in_vmem] * 4,
        scratch_shapes=[
            pltpu.SMEM((NX * NY,), jnp.int32), vmem(TOK, HEADS * HD), vmem(TOK, HEADS * HD),
            vmem(NX, HD, QCOLS), vmem(NX, HD, QCOLS),
            vmem(NY, TOK, HD), vmem(NY, TOK, HD),
            vmem(6 * HD, ALLQ, dtype=BF16), vmem(3 * HD, ALLQ, dtype=BF16),
            vmem(ALLK, 6 * HD, dtype=BF16), vmem(ALLK, 3 * HD, dtype=BF16),
            vmem(2 * HD, ALLK, dtype=BF16), vmem(2 * HD, ALLK, dtype=BF16),
            vmem(2 * HD, ALLQ, dtype=BF16), vmem(2 * HD, ALLQ, dtype=BF16),
            vmem(ALLK, ALLQ), vmem(ALLK, ALLQ),
            vmem(ALLK, ALLQ, dtype=BF16), vmem(ALLK, ALLQ, dtype=BF16),
            vmem(ALLK, ALLQ, dtype=BF16), vmem(ALLK, ALLQ, dtype=BF16),
            vmem(8, ALLQ), vmem(8, ALLQ), vmem(8, ALLQ),
            vmem(NX, 2, ALLQ), vmem(NX, 1, ALLQ), vmem(1, ALLQ),
            vmem(NY, TOK, HD), vmem(NY, TOK, HD),
            vmem(NX, HD, QCOLS), vmem(NX, HD, QCOLS),
            vmem(6, TOK, HD), vmem(2, HALF, HD), vmem(6, TOK, HD), vmem(2, HALF, HD),
            vmem(3, HD, QCOLS), vmem(3, HD, QCOLS),
            dma(5),
            dma(3), dma(3), dma(3), dma(3), dma(8), dma(8), dma(12), dma(12),
            dma(3), dma(3), dma(3), dma(3),
            dma(8), dma(8), dma(12), dma(12), dma(3), dma(3), dma(3), dma(3),
        ],
        compiler_params=pltpu.CompilerParams(
            collective_id=0, has_side_effects=True, vmem_limit_bytes=44 * 1024 * 1024
        ),
    )(*(pltpu.with_memory_space_constraint(a, pltpu.HBM) for a in (block_order, queries, key_rows, value_rows, cotangent)))
    return pl.pallas_call(
        store,
        out_shape=shapes,
        in_specs=[in_vmem] * 4,
        out_specs=[in_hbm] * 4,
        scratch_shapes=[dma(4)],
    )(*(pltpu.with_memory_space_constraint(a, pltpu.VMEM) for a in results))


def solution(mesh):
    spread = P("outer", "inner", None)
    return jax.shard_map(
        body,
        mesh=mesh,
        in_specs=(spread, spread, spread, spread, P()),
        out_specs=(spread, spread, spread, spread),
        check_vma=False,
    )
```
